128 devices in a mesh: gx: 16 (over z, x), gy: 8 (over y, core).
Axes of the slice: x: 4, y: 4, z: 4, core: 2. Of those that a mesh axis runs over, the one named last changes fastest.
Arguments:
- gradient: float32 [137, 512, 1024], P(None, 'gx', 'gy'), may hold values from -6 to 6
- coupling: float32 [137, 137], replicated
- transport: bfloat16 [137, 5, 512, 1024], P(None, None, 'gx', 'gy'), may hold values from 0.049804688 to 0.44921875
- obs_jacobian: bfloat16 [137, 1048576], P(None, ('gx', 'gy')), may hold values from -0.5 to 0.5
- send_cols: int32 [128, 16384], P(('gx', 'gy')), may hold values from -1 to 4095, as said below
- obs_slots: int32 [4, 1048576], P(None, ('gx', 'gy')), may hold values from 0 to 16383, as said below
- obs_weight: float32 [4, 1048576], P(None, ('gx', 'gy')), may hold values from 0.1 to 1
- obs_inst: int32 [1048576], P(('gx', 'gy')), may hold values from 0 to 31, as said below
- innovation: float32 [1048576], P(('gx', 'gy')), may hold values from -6 to 6
- valid_count: int32 [128], P(('gx', 'gy')), may hold values from 2048 to 8192
Outputs:
- sensitivity: float32 [137, 512, 1024], P(None, 'gx', 'gy')
- impact: float32 [1048576], P(('gx', 'gy'))
- inst_total: float32 [32], replicated
The draws below stay inside these ranges and needn't reach their ends.
Inputs may be any that keep to these rules, and one draw needn't show every extreme that they name: `send_cols`: an entry is -1 exactly in the slots beyond a live count of the pair (device, owner); live counts lie between 32 and 128, and reach 128 for some pair. `obs_slots`: every entry names a slot that is not empty in the holder's send_cols for this owner. `obs_inst`: each owner holds observations of four instruments of one group.
All inputs are finite; a program needn't handle non-finite values.
Results may differ from the reference program's by a relative error of at most 0.0032.
Values may be sent and summed in bfloat16 or wider, within the bound.
A program may use at most 256 MiB of HBM per device.

```python
import math
import jax
import jax.numpy as jnp
from jax import lax

L = 137
NI = 32
STEPS = 2
CX = 32
CY = 128
CAP = 128
NOBS_DEV = 8192
RANKS = 128
NX = 512
NY = 1024
NOBS = 1048576
N_GY = 8


def live_counts(key):
    count_key = jax.random.fold_in(key, 11)
    shift_key = jax.random.fold_in(key, 12)
    counts = jax.random.randint(count_key, (RANKS, RANKS), CAP // 4, CAP + 1)
    shift = jax.random.randint(shift_key, (), 0, RANKS)
    target = (jnp.arange(RANKS) + shift) % RANKS
    full_pair = target[:, None] == jnp.arange(RANKS)[None, :]
    return (jnp.where(full_pair, CAP, counts).astype(jnp.int32), full_pair, target)


def draw_coupling(key, part):
    key = jax.random.fold_in(key, 5)
    offdiag = jax.random.normal(key, (L, L), jnp.float32) * 0.5 / math.sqrt(L)
    return jnp.eye(L, dtype=jnp.float32) + offdiag


def draw_send_cols(key, part):
    counts, full_pair, target = live_counts(key)
    key = jax.random.fold_in(key, 1)
    columns = jax.random.randint(key, (RANKS, RANKS, CAP), 0, CX * CY)
    position = jnp.arange(CAP)[None, None, :]
    columns = jnp.where(full_pair[:, :, None] & (position == CAP - 1), CX * CY - 1, columns)
    live = position < counts[:, :, None]
    return jnp.where(live, columns, -1).astype(jnp.int32).reshape(RANKS, RANKS * CAP)


def draw_obs_slots(key, part):
    counts, full_pair, target = live_counts(key)
    key = jax.random.fold_in(key, 2)
    holder_key, slot_key = jax.random.split(key)
    holders = jax.random.randint(holder_key, (4, NOBS), 0, RANKS)
    owners = (jnp.arange(NOBS) // NOBS_DEV)[None, :]
    live = counts[holders, owners]
    within = jax.random.randint(slot_key, (4, NOBS), 0, 1 << 20) % live
    slots = holders * CAP + within
    first_obs = target[RANKS - 1] * NOBS_DEV
    point = jnp.arange(4)[:, None]
    column = jnp.arange(NOBS)[None, :]
    slots = jnp.where((column == first_obs) & (point == 0), RANKS * CAP - 1, slots)
    slots = jnp.where((column == first_obs) & (point == 1), 0, slots)
    return slots.astype(jnp.int32)


def draw_obs_inst(key, part):
    key = jax.random.fold_in(key, 4)
    owners = jnp.arange(NOBS) // NOBS_DEV
    group = owners % (NI // 4)
    member = jax.random.randint(key, (NOBS,), 0, 4)
    return (group * 4 + member).astype(jnp.int32)


def draw_valid_count(key, part):
    key = jax.random.fold_in(key, 3)
    count_key, pick_key = jax.random.split(key)
    counts = jax.random.randint(count_key, (RANKS,), NOBS_DEV // 4, NOBS_DEV + 1)
    chosen = jax.random.randint(pick_key, (), 0, RANKS)
    return jnp.where(jnp.arange(RANKS) == chosen, NOBS_DEV, counts).astype(jnp.int32)


def block_scale(own_key, extent, pieces, least, top_value):
    loudness, own = 1.0, jax.random.fold_in(own_key, 6)
    for dim, parts in pieces:
        draws = jnp.exp(jax.random.uniform(jax.random.fold_in(own, dim), (parts,), jnp.float32, least / len(pieces), top_value / len(pieces)))
        loudness = loudness * jnp.repeat(draws, extent[dim] // parts).reshape([-1 if axis == dim else 1 for axis in range(len(extent))])
    return loudness


def scatter_about(rng, extent, deviation, limit, shards=(), held_as=jnp.bfloat16):
    drawn = jax.random.normal(rng, extent, jnp.float32) * deviation
    if len(shards) > 0:
        drawn = block_scale(rng, extent, shards, -0.22, 0.18) * drawn
    return jnp.clip(drawn, min=-limit, max=limit).astype(held_as)


def setup_inputs(seed: int = 0) -> dict:
    splits = jax.random.split(jax.random.key(seed), 11)
    gradient = scatter_about(splits[0], (L, NX, NY), 1.0, 6.0, ((1, 16), (2, 8)), jnp.float32)
    coupling = draw_coupling(jax.random.fold_in(splits[10], 71), 0)
    transport = jnp.clip(0.049804688 + 0.39941406 * jax.random.uniform(splits[2], (L, 5, NX, NY), jnp.float32) ** block_scale(splits[2], (L, 5, NX, NY), ((2, 16), (3, 8)), -0.2, 0.2), 0.049804688, 0.44921875).astype(jnp.bfloat16)
    obs_jacobian = scatter_about(splits[3], (L, NOBS), L ** -0.5, 0.5, ((1, 128),))
    send_cols = draw_send_cols(jax.random.fold_in(splits[10], 71), 0)
    obs_slots = draw_obs_slots(jax.random.fold_in(splits[10], 71), 0)
    obs_weight = jnp.clip(0.1 + 0.9 * jax.random.uniform(splits[6], (4, NOBS), jnp.float32) ** block_scale(splits[6], (4, NOBS), ((1, 128),), -0.2, 0.2), 0.1, 1.0)
    obs_inst = draw_obs_inst(jax.random.fold_in(splits[10], 71), 0)
    innovation = scatter_about(splits[8], (NOBS,), 1.0, 6.0, ((0, 128),), jnp.float32)
    valid_count = draw_valid_count(jax.random.fold_in(splits[10], 71), 0)
    return {"gradient": gradient, "coupling": coupling, "transport": transport, "obs_jacobian": obs_jacobian, "send_cols": send_cols, "obs_slots": obs_slots, "obs_weight": obs_weight, "obs_inst": obs_inst, "innovation": innovation, "valid_count": valid_count}


def vertical_mix(sensitivity, coupling):
    return jnp.einsum("kl,kxy->lxy", coupling, sensitivity, precision=lax.Precision.HIGHEST)


def spread(padded, coef_pad):
    weights = coef_pad.astype(jnp.float32)
    center = weights[..., 0, 1:-1, 1:-1] * padded[..., 1:-1, 1:-1]
    east = (weights[..., 1, :, :] * padded)[..., :-2, 1:-1]
    west = (weights[..., 2, :, :] * padded)[..., 2:, 1:-1]
    north = (weights[..., 3, :, :] * padded)[..., 1:-1, :-2]
    south = (weights[..., 4, :, :] * padded)[..., 1:-1, 2:]
    return center + east + west + north + south


def level_step(level_pair):
    level_field, level_coef = level_pair
    padded = jnp.pad(level_field, 1)
    coef_pad = jnp.pad(level_coef, ((0, 0), (1, 1), (1, 1)))
    return spread(padded, coef_pad)


def reference(gradient, coupling, transport, obs_jacobian, send_cols, obs_slots, obs_weight, obs_inst, innovation, valid_count):
    sensitivity = gradient
    for repeat in range(STEPS):
        sensitivity = lax.map(level_step, (vertical_mix(sensitivity, coupling), transport))
    rounded = sensitivity.astype(jnp.bfloat16).reshape(L, NX * NY)
    owner = (jnp.arange(NOBS) // NOBS_DEV).astype(jnp.int32)
    holder = obs_slots // CAP
    within = obs_slots % CAP
    local_col = send_cols[holder, owner[None, :] * CAP + within]
    column_ids = ((holder // N_GY) * CX + local_col // CY) * NY + (holder % N_GY) * CY + local_col % CY
    ids_blocks = column_ids.reshape(4, RANKS, NOBS_DEV).transpose(1, 0, 2)
    weight_blocks = obs_weight.reshape(4, RANKS, NOBS_DEV).transpose(1, 0, 2)
    jac_blocks = obs_jacobian.reshape(L, RANKS, NOBS_DEV).transpose(1, 0, 2)
    innov_blocks = innovation.reshape(RANKS, NOBS_DEV)

    def owner_impact(pack):
        ids, weights, jacobian, innov_part, count = pack
        gathered = jnp.take(rounded, ids, axis=1)
        interp = jnp.sum(weights[None] * gathered.astype(jnp.float32), axis=1)
        sens_obs = jnp.sum(jacobian.astype(jnp.float32) * interp, axis=0)
        active = jnp.arange(NOBS_DEV) < count
        values = innov_part * sens_obs
        return jnp.where(active, values, jnp.zeros_like(values))

    impact = lax.map(owner_impact, (ids_blocks, weight_blocks, jac_blocks, innov_blocks, valid_count)).reshape(NOBS)
    inst_total = jax.ops.segment_sum(impact, obs_inst, num_segments=NI)
    return sensitivity, impact, inst_total
```

```python
import jax
import jax.numpy as jnp
from jax import lax
from jax.experimental import pallas as pl
from jax.experimental.pallas import tpu as pltpu
from jax.sharding import PartitionSpec as P

NI = 32
STEPS = 2
LANES = 128
MAIN = 128
TAIL = 16
BLOCK = MAIN + TAIL
GROUP = 8
STRIDE = 37
MESH = pl.DeviceIdType.MESH
VMEM = pl.BlockSpec(memory_space=pltpu.VMEM)
SMEM = pl.BlockSpec(memory_space=pltpu.SMEM)
MIB = 1024 * 1024


def padded_2(x, sides, width):
    for axis, dim in sides:
        size, length = (lax.axis_size(axis), x.shape[dim])
        up = [(i, (i + 1) % size) for i in range(size - 1)]
        down = [(j, i) for i, j in up]
        last = lax.slice_in_dim(x, length - width, length, axis=dim)
        leading = lax.slice_in_dim(x, 0, width, axis=dim)
        before = lax.ppermute(last, axis, up)
        after = lax.ppermute(leading, axis, down)
        x = jnp.concatenate([before, x, after], axis=dim)
    return x


def vertical_mix(sensitivity, coupling):
    return jnp.einsum("kl,kxy->lxy", coupling, sensitivity, precision=lax.Precision.HIGHEST)


def spread(padded, coef_pad):
    weights = coef_pad.astype(jnp.float32)
    center = weights[..., 0, 1:-1, 1:-1] * padded[..., 1:-1, 1:-1]
    east = (weights[..., 1, :, :] * padded)[..., :-2, 1:-1]
    west = (weights[..., 2, :, :] * padded)[..., 2:, 1:-1]
    north = (weights[..., 3, :, :] * padded)[..., 1:-1, :-2]
    south = (weights[..., 4, :, :] * padded)[..., 1:-1, 2:]
    return center + east + west + north + south


def extend(sensitivity, rim_depth):
    return padded_2(sensitivity, (("gx", 1), ("gy", 2)), rim_depth)


def transport_steps(gradient, coupling, transport):
    sensitivity = gradient
    rim_depth = 1
    coef_wide = padded_2(transport, (("gx", 2), ("gy", 3)), rim_depth)
    for repeat in range(STEPS):
        sensitivity = spread(extend(vertical_mix(sensitivity, coupling), 1), coef_wide)
    return sensitivity


def identity(rows, dtype):
    row = lax.broadcasted_iota(jnp.int32, (rows, LANES), 0)
    col = lax.broadcasted_iota(jnp.int32, (rows, LANES), 1)
    return (row == col).astype(dtype)


def dot_nt(a, b):
    return lax.dot_general(a, b, (((1,), (1,)), ((), ())), preferred_element_type=jnp.float32)


def peer(step):
    gx, gy = lax.axis_index("gx"), lax.axis_index("gy")
    z, x, y, core = gx // 4, lax.rem(gx, 4), gy // 2, lax.rem(gy, 2)
    dz, dx, dy, dc = lax.rem(step, 4), lax.rem(step // 4, 4), lax.rem(step // 16, 4), step // 64
    return (
        lax.rem(z + dz, 4) * 4 + lax.rem(x + dx, 4),
        lax.rem(y + dy, 4) * 2 + lax.rem(core + dc, 2),
    )


def exchange_kernel(levels, columns, field, received, table, ga, gb, outgoing, send_sem, recv_sem, own_sem):
    gx, gy = lax.axis_index("gx"), lax.axis_index("gy")
    me = gx * 8 + gy
    ranks = received.shape[0]
    barrier = pltpu.get_barrier_semaphore()

    @pl.loop(1, ranks)
    def _(k):
        pl.semaphore_signal(barrier, inc=1, device_id=peer(k), device_id_type=MESH)

    rows_x = field.shape[0] // levels
    eye = identity(LANES, jnp.bfloat16)

    @pl.loop(0, rows_x, unroll=4)
    def _(x):
        slab = field[pl.ds(x, levels, stride=rows_x), :]
        tail = jnp.concatenate([slab[MAIN:levels], jnp.zeros((2 * MAIN - levels, LANES), jnp.float32)], axis=0)
        base = pl.multiple_of(x * 2 * LANES, 2 * LANES)
        table[pl.ds(base, LANES, stride=2), :] = dot_nt(eye, slab[:MAIN].astype(jnp.bfloat16))
        table[pl.ds(base + 1, LANES, stride=2), :] = dot_nt(eye, tail.astype(jnp.bfloat16))

    pick = identity(TAIL, jnp.bfloat16)
    pl.semaphore_wait(barrier, ranks - 1)

    def step_at(k):
        return lax.rem((k + 1) * STRIDE, ranks)

    def owner_at(k):
        tx, ty = peer(step_at(k))
        return tx * 8 + ty

    def copy_for(k):
        step = step_at(k)
        tx, ty = peer(step)
        return pltpu.make_async_remote_copy(
            src_ref=outgoing.at[tx * 8 + ty],
            dst_ref=received.at[me],
            send_sem=send_sem.at[step],
            recv_sem=recv_sem.at[step],
            device_id=(tx, ty),
            device_id_type=MESH,
        )

    def gather(k, rows, first, count):
        base = owner_at(k) * LANES
        for i in range(first, first + count, GROUP):
            got = [table[pl.ds(columns[base + i + j], 2), :] for j in range(GROUP)]
            for j in range(GROUP):
                rows[pl.ds((i + j) * 2, 2), :] = got[j]

    def pack(k, rows, next_k, next_rows):
        owner = owner_at(k)
        main = rows[pl.ds(0, LANES, stride=2), :].astype(jnp.bfloat16)
        tail = rows[pl.ds(1, LANES, stride=2), :].astype(jnp.bfloat16)
        packed = dot_nt(pick, tail)
        gather(next_k, next_rows, 0, LANES)
        outgoing[owner, 0:MAIN, :] = main
        outgoing[owner, MAIN:BLOCK, :] = packed.astype(jnp.bfloat16)

    gather(0, ga, 0, LANES)

    @pl.loop(0, ranks // 2)
    def _(t):
        k = t * 2
        pack(k, ga, k + 1, gb)
        copy_for(k).start()
        pack(k + 1, gb, jnp.minimum(k + 2, ranks - 1), ga)

        @pl.when(k + 1 < ranks - 1)
        def _():
            copy_for(k + 1).start()

    own = pltpu.make_async_copy(outgoing.at[me], received.at[me], own_sem)
    own.start()

    @pl.loop(0, ranks - 1)
    def _(k):
        copy_for(k).wait()

    own.wait()


def exchange(columns, field, ranks):
    levels, rows_x, lanes = field.shape
    flat = field.reshape(levels * rows_x, lanes)
    block = jax.ShapeDtypeStruct((ranks, BLOCK, LANES), jnp.bfloat16)

    def kernel(*refs):
        exchange_kernel(levels, *refs)

    return pl.pallas_call(
        kernel,
        out_shape=block,
        in_specs=[SMEM, VMEM],
        out_specs=VMEM,
        scratch_shapes=[
            pltpu.VMEM((rows_x * lanes * 2, LANES), jnp.float32),
            pltpu.VMEM((2 * LANES, LANES), jnp.float32),
            pltpu.VMEM((2 * LANES, LANES), jnp.float32),
            pltpu.VMEM(block.shape, block.dtype),
            pltpu.SemaphoreType.DMA((ranks,)),
            pltpu.SemaphoreType.DMA((ranks,)),
            pltpu.SemaphoreType.DMA,
        ],
        compiler_params=pltpu.CompilerParams(collective_id=1, has_side_effects=True, vmem_limit_bytes=40 * MIB),
        name="exchange",
    )(columns, flat)


def impact_kernel(slots, valid, received, jac, weight, innovation, inst, impact, part, table, ga, gb):
    levels, holders, chunks = jac.shape[0], received.shape[0], impact.shape[0]
    eye = identity(LANES, jnp.int32) == 1
    spread_tail = identity(TAIL, jnp.bfloat16)

    @pl.loop(0, holders, unroll=8)
    def _(h):
        base = pl.multiple_of(h * 2 * LANES, 2 * LANES)
        table[pl.ds(base, LANES, stride=2), :] = received[h, 0:MAIN, :].astype(jnp.float32)
        table[pl.ds(base + 1, LANES, stride=2), :] = lax.dot_general(
            received[h, MAIN:BLOCK, :], spread_tail, (((0,), (0,)), ((), ())), preferred_element_type=jnp.float32
        )

    part[...] = jnp.zeros_like(part)
    lane = lax.broadcasted_iota(jnp.int32, (1, LANES), 1)
    points = 4
    rows_per = points * LANES

    def gather(j, rows, first, count):
        for i in range(first, first + count, GROUP):
            got = [table[pl.ds(slots[j * rows_per + i + k], 2), :] for k in range(GROUP)]
            for k in range(GROUP):
                rows[pl.ds((i + k) * 2, 2), :] = got[k]

    def work(j, rows, next_j, next_rows):
        col = pl.multiple_of(j * LANES, LANES)
        tail = jnp.concatenate(
            [
                jac[MAIN:levels, pl.ds(col, LANES)].astype(jnp.float32),
                jnp.zeros((BLOCK - levels, LANES), jnp.float32),
            ],
            axis=0,
        ).astype(jnp.bfloat16)
        profile = jnp.concatenate(
            [jac[0:MAIN, pl.ds(col, LANES)], tail, jnp.zeros((2 * MAIN - BLOCK, LANES), jnp.bfloat16)], axis=0
        )
        total = jnp.zeros((1, LANES), jnp.float32)
        for c in range(points):
            main = rows[pl.ds(c * 2 * LANES, LANES, stride=2), :].astype(jnp.bfloat16)
            rest = rows[pl.ds(c * 2 * LANES + 1, LANES, stride=2), :].astype(jnp.bfloat16)
            products = jnp.dot(
                jnp.concatenate([main, rest], axis=1), profile, preferred_element_type=jnp.float32
            )
            gather(next_j, next_rows, c * LANES, LANES // 2)
            diagonal = jnp.sum(jnp.where(eye, products, 0.0), axis=0, keepdims=True)
            total = total + diagonal * weight[c : c + 1, pl.ds(col, LANES)]
            gather(next_j, next_rows, c * LANES + LANES // 2, LANES // 2)
        value = innovation[pl.ds(j, 1), :] * total
        value = jnp.where(lane + j * LANES < valid[0], value, 0.0)
        impact[pl.ds(j, 1), :] = value
        same = lax.broadcasted_iota(jnp.int32, (NI, LANES), 0) == inst[pl.ds(j, 1), :]
        part[...] += jnp.where(same, value, 0.0)

    gather(0, ga, 0, rows_per)

    @pl.loop(0, chunks // 2)
    def _(t):
        j = t * 2
        work(j, ga, j + 1, gb)
        work(j + 1, gb, jnp.minimum(j + 2, chunks - 1), ga)


def impacts(slots, valid, received, jac, weight, innovation, inst):
    count, holders = innovation.shape[0], received.shape[0]
    chunks = count // LANES
    slots = (slots * 2).reshape(4, chunks, LANES).transpose(1, 0, 2).reshape(4 * count)
    impact, part = pl.pallas_call(
        impact_kernel,
        out_shape=(
            jax.ShapeDtypeStruct((chunks, LANES), jnp.float32),
            jax.ShapeDtypeStruct((NI, LANES), jnp.float32),
        ),
        in_specs=[SMEM, SMEM] + [VMEM] * 5,
        out_specs=(VMEM, VMEM),
        scratch_shapes=[
            pltpu.VMEM((holders * 2 * LANES, LANES), jnp.float32),
            pltpu.VMEM((4 * 2 * LANES, LANES), jnp.float32),
            pltpu.VMEM((4 * 2 * LANES, LANES), jnp.float32),
        ],
        compiler_params=pltpu.CompilerParams(vmem_limit_bytes=48 * MIB),
        name="impacts",
    )(slots, valid, received, jac, weight, innovation.reshape(chunks, LANES), inst.reshape(chunks, LANES))
    return impact.reshape(count), part


def total_kernel(part, total, first, second, send_sem, recv_sem):
    gx, gy = lax.axis_index("gx"), lax.axis_index("gy")
    nx, ny = first.shape[0], second.shape[0]
    barrier = pltpu.get_barrier_semaphore()
    for k in range(1, ny):
        pl.semaphore_signal(barrier, inc=1, device_id=(gx, lax.rem(gy + k, ny)), device_id_type=MESH)
    for k in range(1, nx):
        pl.semaphore_signal(barrier, inc=1, device_id=(lax.rem(gx + k, nx), gy), device_id_type=MESH)
    rows = lax.dot_general(
        jnp.ones((8, LANES), jnp.float32),
        part[...],
        (((1,), (1,)), ((), ())),
        precision=lax.Precision.HIGHEST,
        preferred_element_type=jnp.float32,
    )
    own = jnp.concatenate([rows, jnp.zeros((8, LANES - NI), jnp.float32)], axis=1)
    pl.semaphore_wait(barrier, nx + ny - 2)

    def share(value, slots, size, me, coords, base):
        slots[me] = value
        copies = [
            pltpu.make_async_remote_copy(
                src_ref=slots.at[me],
                dst_ref=slots.at[me],
                send_sem=send_sem.at[base + k],
                recv_sem=recv_sem.at[base + k],
                device_id=coords(lax.rem(me + k, size)),
                device_id_type=MESH,
            )
            for k in range(1, size)
        ]
        for copy in copies:
            copy.start()
        for copy in copies:
            copy.wait()
        out = slots[0]
        for k in range(1, size):
            out = out + slots[k]
        return out

    across = share(own, second, ny, gy, lambda i: (gx, i), 0)
    total[...] = share(across, first, nx, gx, lambda i: (i, gy), ny)


def instrument_totals(part, nx, ny):
    total = pl.pallas_call(
        total_kernel,
        out_shape=jax.ShapeDtypeStruct((8, LANES), jnp.float32),
        in_specs=[VMEM],
        out_specs=VMEM,
        scratch_shapes=[
            pltpu.VMEM((nx, 8, LANES), jnp.float32),
            pltpu.VMEM((ny, 8, LANES), jnp.float32),
            pltpu.SemaphoreType.DMA((nx + ny,)),
            pltpu.SemaphoreType.DMA((nx + ny,)),
        ],
        compiler_params=pltpu.CompilerParams(collective_id=2, has_side_effects=True),
        name="totals",
    )(part)
    return total[0, :NI]


def body(
    gradient,
    coupling,
    transport,
    obs_jacobian,
    send_cols,
    obs_slots,
    obs_weight,
    obs_inst,
    innovation,
    valid_count,
):
    nx, ny = lax.axis_size("gx"), lax.axis_size("gy")
    sensitivity = transport_steps(gradient, coupling, transport)
    columns = jnp.maximum(send_cols[0], 0) * 2
    received = exchange(columns, sensitivity, nx * ny)
    impact, part = impacts(
        obs_slots, valid_count, received, obs_jacobian, obs_weight, innovation, obs_inst
    )
    return (sensitivity, impact, instrument_totals(part, nx, ny))


def solution(mesh):
    placed = (
        P(None, "gx", "gy"),
        P(),
        P(None, None, "gx", "gy"),
        P(None, ("gx", "gy")),
        P(("gx", "gy"), None),
        P(None, ("gx", "gy")),
        P(None, ("gx", "gy")),
        P(("gx", "gy")),
        P(("gx", "gy")),
        P(("gx", "gy")),
    )
    return jax.shard_map(
        body,
        mesh=mesh,
        in_specs=placed,
        out_specs=(P(None, "gx", "gy"), P(("gx", "gy")), P()),
        check_vma=False,
    )
```

```python
import jax
import jax.numpy as jnp
from jax import lax
from jax.experimental import pallas as pl
from jax.experimental.pallas import tpu as pltpu
from jax.sharding import PartitionSpec as P

NI = 32
STEPS = 2
LANES = 128
MAIN = 128
TAIL = 16
BLOCK = MAIN + TAIL
GROUP = 8
STRIDE = 37
MESH = pl.DeviceIdType.MESH
VMEM = pl.BlockSpec(memory_space=pltpu.VMEM)
SMEM = pl.BlockSpec(memory_space=pltpu.SMEM)
MIB = 1024 * 1024


def identity(rows, dtype):
    row = lax.broadcasted_iota(jnp.int32, (rows, LANES), 0)
    col = lax.broadcasted_iota(jnp.int32, (rows, LANES), 1)
    return (row == col).astype(dtype)


def dot_nt(a, b):
    return lax.dot_general(a, b, (((1,), (1,)), ((), ())), preferred_element_type=jnp.float32)


def peer(step):
    gx, gy = lax.axis_index("gx"), lax.axis_index("gy")
    z, x, y, core = gx // 4, lax.rem(gx, 4), gy // 2, lax.rem(gy, 2)
    dz, dx, dy, dc = lax.rem(step, 4), lax.rem(step // 4, 4), lax.rem(step // 16, 4), step // 64
    return (
        lax.rem(z + dz, 4) * 4 + lax.rem(x + dx, 4),
        lax.rem(y + dy, 4) * 2 + lax.rem(core + dc, 2),
    )


def split(value):
    high = value.astype(jnp.bfloat16)
    return high, (value - high.astype(jnp.float32)).astype(jnp.bfloat16)


def vertical_mix(levels, rows_x, coupling_t, source, mixed):
    padded = coupling_t.shape[0]
    stacked = jnp.concatenate(split(coupling_t[...]), axis=0)
    pad = jnp.zeros((padded - levels, 2 * LANES), jnp.float32)

    @pl.loop(0, rows_x // 2, unroll=2)
    def _(t):
        x = 2 * t
        pair = jnp.concatenate(
            [source[pl.ds(x, levels, stride=rows_x), :], source[pl.ds(x + 1, levels, stride=rows_x), :]], axis=1
        )
        high, low = split(jnp.concatenate([pair, pad], axis=0))
        both = jnp.dot(stacked, high, preferred_element_type=jnp.float32)
        out = both[:padded] + (
            both[padded:] + jnp.dot(stacked[:padded], low, preferred_element_type=jnp.float32)
        )
        mixed[pl.ds(x, levels, stride=rows_x), :] = out[:levels, :LANES]
        mixed[pl.ds(x + 1, levels, stride=rows_x), :] = out[:levels, LANES:]


def spread(levels, rows_x, transport, mixed, out, row_edge, col_edge):
    row = lax.broadcasted_iota(jnp.int32, (rows_x, LANES), 0)
    lane = lax.broadcasted_iota(jnp.int32, (rows_x, LANES), 1)
    col_edge[...] = jnp.zeros_like(col_edge)

    @pl.loop(0, levels)
    def _(l):
        here = pl.ds(pl.multiple_of(l * rows_x, rows_x), rows_x)
        u = mixed[here, :]
        part = [transport[l, k].astype(jnp.float32) * u for k in range(5)]
        down = pltpu.roll(part[1], 1, 0)
        up = pltpu.roll(part[2], rows_x - 1, 0)
        right = pltpu.roll(part[3], 1, 1)
        left = pltpu.roll(part[4], LANES - 1, 1)
        row_edge[0, pl.ds(l, 1), :] = down[0:1]
        row_edge[1, pl.ds(l, 1), :] = up[rows_x - 1 : rows_x]
        bank, spot = l // LANES, lax.rem(l, LANES)
        at = lane == spot
        col_edge[0, bank] = jnp.where(at, pltpu.roll(right, spot, 1), col_edge[0, bank])
        col_edge[1, bank] = jnp.where(at, pltpu.roll(left, lax.rem(spot + 1, LANES), 1), col_edge[1, bank])
        total = part[0] + jnp.where(row == 0, 0.0, down) + jnp.where(row == rows_x - 1, 0.0, up)
        total = total + jnp.where(lane == 0, 0.0, right) + jnp.where(lane == LANES - 1, 0.0, left)
        out[here, :] = total


def add_edges(levels, rows_x, out, row_halo, col_halo, gx, gy, nx, ny):
    lane = lax.broadcasted_iota(jnp.int32, (rows_x, LANES), 1)
    first, last = pl.ds(0, levels, stride=rows_x), pl.ds(rows_x - 1, levels, stride=rows_x)
    out[first, :] = out[first, :] + jnp.where(gx > 0, row_halo[0, 0:levels, :], 0.0)
    out[last, :] = out[last, :] + jnp.where(gx < nx - 1, row_halo[1, 0:levels, :], 0.0)
    at_first = (lane == 0) & (gy > 0)
    at_last = (lane == LANES - 1) & (gy < ny - 1)

    @pl.loop(0, levels)
    def _(l):
        here = pl.ds(pl.multiple_of(l * rows_x, rows_x), rows_x)
        bank, spot = l // LANES, lax.rem(l, LANES)
        before = pltpu.roll(col_halo[0, bank], lax.rem(LANES - spot, LANES), 1)
        after = pltpu.roll(col_halo[1, bank], LANES - 1 - spot, 1)
        out[here, :] = out[here, :] + jnp.where(at_first, before, 0.0) + jnp.where(at_last, after, 0.0)


def exchange_kernel(
    levels,
    columns,
    gradient,
    coupling_t,
    transport,
    field,
    received,
    mixed,
    row_edge,
    col_edge,
    row_halo,
    col_halo,
    table,
    ga,
    gb,
    outgoing,
    edge_send,
    edge_recv,
    send_sem,
    recv_sem,
    own_sem,
):
    gx, gy = lax.axis_index("gx"), lax.axis_index("gy")
    nx, ny = lax.axis_size("gx"), lax.axis_size("gy")
    me = gx * ny + gy
    ranks = received.shape[0]
    barrier = pltpu.get_barrier_semaphore()

    @pl.loop(1, ranks)
    def _(k):
        pl.semaphore_signal(barrier, inc=1, device_id=peer(k), device_id_type=MESH)

    rows_x = field.shape[0] // levels
    sides = (
        (row_edge, row_halo, 0, (lax.rem(gx + 1, nx), gy)),
        (row_edge, row_halo, 1, (lax.rem(gx + nx - 1, nx), gy)),
        (col_edge, col_halo, 0, (gx, lax.rem(gy + 1, ny))),
        (col_edge, col_halo, 1, (gx, lax.rem(gy + ny - 1, ny))),
    )
    for step in range(STEPS):
        vertical_mix(levels, rows_x, coupling_t, gradient if step == 0 else field, mixed)
        spread(levels, rows_x, transport, mixed, field, row_edge.at[step], col_edge.at[step])
        if step == 0:
            pl.semaphore_wait(barrier, ranks - 1)
        copies = [
            pltpu.make_async_remote_copy(
                src_ref=edge.at[step, side],
                dst_ref=halo.at[step, side],
                send_sem=edge_send.at[step, i],
                recv_sem=edge_recv.at[step, i],
                device_id=device,
                device_id_type=MESH,
            )
            for i, (edge, halo, side, device) in enumerate(sides)
        ]
        for copy in copies:
            copy.start()
        for copy in copies:
            copy.wait()
        add_edges(levels, rows_x, field, row_halo.at[step], col_halo.at[step], gx, gy, nx, ny)

    eye = identity(LANES, jnp.bfloat16)

    @pl.loop(0, rows_x, unroll=4)
    def _(x):
        slab = field[pl.ds(x, levels, stride=rows_x), :]
        tail = jnp.concatenate([slab[MAIN:levels], jnp.zeros((2 * MAIN - levels, LANES), jnp.float32)], axis=0)
        base = pl.multiple_of(x * 2 * LANES, 2 * LANES)
        table[pl.ds(base, LANES, stride=2), :] = dot_nt(eye, slab[:MAIN].astype(jnp.bfloat16))
        table[pl.ds(base + 1, LANES, stride=2), :] = dot_nt(eye, tail.astype(jnp.bfloat16))

    pick = identity(TAIL, jnp.bfloat16)

    def step_at(k):
        return lax.rem((k + 1) * STRIDE, ranks)

    def owner_at(k):
        tx, ty = peer(step_at(k))
        return tx * ny + ty

    def copy_for(k):
        step = step_at(k)
        tx, ty = peer(step)
        return pltpu.make_async_remote_copy(
            src_ref=outgoing.at[tx * ny + ty],
            dst_ref=received.at[me],
            send_sem=send_sem.at[step],
            recv_sem=recv_sem.at[step],
            device_id=(tx, ty),
            device_id_type=MESH,
        )

    def gather(k, rows, first, count):
        base = owner_at(k) * LANES
        for i in range(first, first + count, GROUP):
            got = [table[pl.ds(columns[base + i + j], 2), :] for j in range(GROUP)]
            for j in range(GROUP):
                rows[pl.ds((i + j) * 2, 2), :] = got[j]

    def pack(k, rows, next_k, next_rows):
        owner = owner_at(k)
        main = rows[pl.ds(0, LANES, stride=2), :].astype(jnp.bfloat16)
        tail = rows[pl.ds(1, LANES, stride=2), :].astype(jnp.bfloat16)
        packed = dot_nt(pick, tail)
        gather(next_k, next_rows, 0, LANES)
        outgoing[owner, 0:MAIN, :] = main
        outgoing[owner, MAIN:BLOCK, :] = packed.astype(jnp.bfloat16)

    gather(0, ga, 0, LANES)

    @pl.loop(0, ranks // 2)
    def _(t):
        k = t * 2
        pack(k, ga, k + 1, gb)
        copy_for(k).start()
        pack(k + 1, gb, jnp.minimum(k + 2, ranks - 1), ga)

        @pl.when(k + 1 < ranks - 1)
        def _():
            copy_for(k + 1).start()

    own = pltpu.make_async_copy(outgoing.at[me], received.at[me], own_sem)
    own.start()

    @pl.loop(0, ranks - 1)
    def _(k):
        copy_for(k).wait()

    own.wait()


def exchange(columns, gradient, coupling, transport, ranks):
    levels, rows_x, lanes = gradient.shape
    flat = gradient.reshape(levels * rows_x, lanes)
    padded = -(-levels // TAIL) * TAIL
    coupling_t = jnp.pad(coupling.T, ((0, padded - levels), (0, padded - levels)))
    block = jax.ShapeDtypeStruct((ranks, BLOCK, LANES), jnp.bfloat16)
    row_edges = pltpu.VMEM((STEPS, 2, padded, LANES), jnp.float32)
    col_edges = pltpu.VMEM((STEPS, 2, 2, rows_x, LANES), jnp.float32)

    def kernel(*refs):
        exchange_kernel(levels, *refs)

    field, received = pl.pallas_call(
        kernel,
        out_shape=(jax.ShapeDtypeStruct(flat.shape, jnp.float32), block),
        in_specs=[SMEM, VMEM, VMEM, VMEM],
        out_specs=(VMEM, VMEM),
        scratch_shapes=[
            pltpu.VMEM(flat.shape, jnp.float32),
            row_edges,
            col_edges,
            row_edges,
            col_edges,
            pltpu.VMEM((rows_x * lanes * 2, LANES), jnp.float32),
            pltpu.VMEM((2 * LANES, LANES), jnp.float32),
            pltpu.VMEM((2 * LANES, LANES), jnp.float32),
            pltpu.VMEM(block.shape, block.dtype),
            pltpu.SemaphoreType.DMA((STEPS, 4)),
            pltpu.SemaphoreType.DMA((STEPS, 4)),
            pltpu.SemaphoreType.DMA((ranks,)),
            pltpu.SemaphoreType.DMA((ranks,)),
            pltpu.SemaphoreType.DMA,
        ],
        compiler_params=pltpu.CompilerParams(collective_id=1, has_side_effects=True, vmem_limit_bytes=48 * MIB),
        name="exchange",
    )(columns, flat, coupling_t, transport)
    return field.reshape(gradient.shape), received


def impact_kernel(slots, valid, received, jac, weight, innovation, inst, impact, part, table, ga, gb):
    levels, holders, chunks = jac.shape[0], received.shape[0], impact.shape[0]
    eye = identity(LANES, jnp.int32) == 1
    spread_tail = identity(TAIL, jnp.bfloat16)

    @pl.loop(0, holders, unroll=8)
    def _(h):
        base = pl.multiple_of(h * 2 * LANES, 2 * LANES)
        table[pl.ds(base, LANES, stride=2), :] = received[h, 0:MAIN, :].astype(jnp.float32)
        table[pl.ds(base + 1, LANES, stride=2), :] = lax.dot_general(
            received[h, MAIN:BLOCK, :], spread_tail, (((0,), (0,)), ((), ())), preferred_element_type=jnp.float32
        )

    part[...] = jnp.zeros_like(part)
    lane = lax.broadcasted_iota(jnp.int32, (1, LANES), 1)
    points = 4
    rows_per = points * LANES

    def gather(j, rows, first, count):
        for i in range(first, first + count, GROUP):
            got = [table[pl.ds(slots[j * rows_per + i + k], 2), :] for k in range(GROUP)]
            for k in range(GROUP):
                rows[pl.ds((i + k) * 2, 2), :] = got[k]

    def work(j, rows, next_j, next_rows):
        col = pl.multiple_of(j * LANES, LANES)
        tail = jnp.concatenate(
            [
                jac[MAIN:levels, pl.ds(col, LANES)].astype(jnp.float32),
                jnp.zeros((BLOCK - levels, LANES), jnp.float32),
            ],
            axis=0,
        ).astype(jnp.bfloat16)
        profile = jnp.concatenate(
            [jac[0:MAIN, pl.ds(col, LANES)], tail, jnp.zeros((2 * MAIN - BLOCK, LANES), jnp.bfloat16)], axis=0
        )
        total = jnp.zeros((1, LANES), jnp.float32)
        for c in range(points):
            main = rows[pl.ds(c * 2 * LANES, LANES, stride=2), :].astype(jnp.bfloat16)
            rest = rows[pl.ds(c * 2 * LANES + 1, LANES, stride=2), :].astype(jnp.bfloat16)
            products = jnp.dot(
                jnp.concatenate([main, rest], axis=1), profile, preferred_element_type=jnp.float32
            )
            gather(next_j, next_rows, c * LANES, LANES // 2)
            diagonal = jnp.sum(jnp.where(eye, products, 0.0), axis=0, keepdims=True)
            total = total + diagonal * weight[c : c + 1, pl.ds(col, LANES)]
            gather(next_j, next_rows, c * LANES + LANES // 2, LANES // 2)
        value = innovation[pl.ds(j, 1), :] * total
        value = jnp.where(lane + j * LANES < valid[0], value, 0.0)
        impact[pl.ds(j, 1), :] = value
        same = lax.broadcasted_iota(jnp.int32, (NI, LANES), 0) == inst[pl.ds(j, 1), :]
        part[...] += jnp.where(same, value, 0.0)

    gather(0, ga, 0, rows_per)

    @pl.loop(0, chunks // 2)
    def _(t):
        j = t * 2
        work(j, ga, j + 1, gb)
        work(j + 1, gb, jnp.minimum(j + 2, chunks - 1), ga)


def impacts(slots, valid, received, jac, weight, innovation, inst):
    count, holders = innovation.shape[0], received.shape[0]
    chunks = count // LANES
    slots = (slots * 2).reshape(4, chunks, LANES).transpose(1, 0, 2).reshape(4 * count)
    impact, part = pl.pallas_call(
        impact_kernel,
        out_shape=(
            jax.ShapeDtypeStruct((chunks, LANES), jnp.float32),
            jax.ShapeDtypeStruct((NI, LANES), jnp.float32),
        ),
        in_specs=[SMEM, SMEM] + [VMEM] * 5,
        out_specs=(VMEM, VMEM),
        scratch_shapes=[
            pltpu.VMEM((holders * 2 * LANES, LANES), jnp.float32),
            pltpu.VMEM((4 * 2 * LANES, LANES), jnp.float32),
            pltpu.VMEM((4 * 2 * LANES, LANES), jnp.float32),
        ],
        compiler_params=pltpu.CompilerParams(vmem_limit_bytes=48 * MIB),
        name="impacts",
    )(slots, valid, received, jac, weight, innovation.reshape(chunks, LANES), inst.reshape(chunks, LANES))
    return impact.reshape(count), part


def total_kernel(part, total, first, second, send_sem, recv_sem):
    gx, gy = lax.axis_index("gx"), lax.axis_index("gy")
    nx, ny = first.shape[0], second.shape[0]
    barrier = pltpu.get_barrier_semaphore()
    for k in range(1, ny):
        pl.semaphore_signal(barrier, inc=1, device_id=(gx, lax.rem(gy + k, ny)), device_id_type=MESH)
    for k in range(1, nx):
        pl.semaphore_signal(barrier, inc=1, device_id=(lax.rem(gx + k, nx), gy), device_id_type=MESH)
    rows = lax.dot_general(
        jnp.ones((8, LANES), jnp.float32),
        part[...],
        (((1,), (1,)), ((), ())),
        precision=lax.Precision.HIGHEST,
        preferred_element_type=jnp.float32,
    )
    own = jnp.concatenate([rows, jnp.zeros((8, LANES - NI), jnp.float32)], axis=1)
    pl.semaphore_wait(barrier, nx + ny - 2)

    def share(value, slots, size, me, coords, base):
        slots[me] = value
        copies = [
            pltpu.make_async_remote_copy(
                src_ref=slots.at[me],
                dst_ref=slots.at[me],
                send_sem=send_sem.at[base + k],
                recv_sem=recv_sem.at[base + k],
                device_id=coords(lax.rem(me + k, size)),
                device_id_type=MESH,
            )
            for k in range(1, size)
        ]
        for copy in copies:
            copy.start()
        for copy in copies:
            copy.wait()
        out = slots[0]
        for k in range(1, size):
            out = out + slots[k]
        return out

    across = share(own, second, ny, gy, lambda i: (gx, i), 0)
    total[...] = share(across, first, nx, gx, lambda i: (i, gy), ny)


def instrument_totals(part, nx, ny):
    total = pl.pallas_call(
        total_kernel,
        out_shape=jax.ShapeDtypeStruct((8, LANES), jnp.float32),
        in_specs=[VMEM],
        out_specs=VMEM,
        scratch_shapes=[
            pltpu.VMEM((nx, 8, LANES), jnp.float32),
            pltpu.VMEM((ny, 8, LANES), jnp.float32),
            pltpu.SemaphoreType.DMA((nx + ny,)),
            pltpu.SemaphoreType.DMA((nx + ny,)),
        ],
        compiler_params=pltpu.CompilerParams(collective_id=2, has_side_effects=True),
        name="totals",
    )(part)
    return total[0, :NI]


def body(
    gradient,
    coupling,
    transport,
    obs_jacobian,
    send_cols,
    obs_slots,
    obs_weight,
    obs_inst,
    innovation,
    valid_count,
):
    nx, ny = lax.axis_size("gx"), lax.axis_size("gy")
    columns = jnp.maximum(send_cols[0], 0) * 2
    sensitivity, received = exchange(columns, gradient, coupling, transport, nx * ny)
    impact, part = impacts(
        obs_slots, valid_count, received, obs_jacobian, obs_weight, innovation, obs_inst
    )
    return (sensitivity, impact, instrument_totals(part, nx, ny))


def solution(mesh):
    placed = (
        P(None, "gx", "gy"),
        P(),
        P(None, None, "gx", "gy"),
        P(None, ("gx", "gy")),
        P(("gx", "gy"), None),
        P(None, ("gx", "gy")),
        P(None, ("gx", "gy")),
        P(("gx", "gy")),
        P(("gx", "gy")),
        P(("gx", "gy")),
    )
    return jax.shard_map(
        body,
        mesh=mesh,
        in_specs=placed,
        out_specs=(P(None, "gx", "gy"), P(("gx", "gy")), P()),
        check_vma=False,
    )
```

```python
import jax
import jax.numpy as jnp
from jax import lax
from jax.experimental import pallas as pl
from jax.experimental.pallas import tpu as pltpu
from jax.sharding import PartitionSpec as P

NI = 32
STEPS = 2
LANES = 128
MAIN = 128
TAIL = 16
BLOCK = MAIN + TAIL
GROUP = 8
WIDE = 8
STRIDE = 37
MESH = pl.DeviceIdType.MESH
VMEM = pl.BlockSpec(memory_space=pltpu.VMEM)
SMEM = pl.BlockSpec(memory_space=pltpu.SMEM)
MIB = 1024 * 1024


def identity(rows, dtype):
    row = lax.broadcasted_iota(jnp.int32, (rows, LANES), 0)
    col = lax.broadcasted_iota(jnp.int32, (rows, LANES), 1)
    return (row == col).astype(dtype)


def dot_nt(a, b):
    return lax.dot_general(a, b, (((1,), (1,)), ((), ())), preferred_element_type=jnp.float32)


def peer(step):
    gx, gy = lax.axis_index("gx"), lax.axis_index("gy")
    z, x, y, core = gx // 4, lax.rem(gx, 4), gy // 2, lax.rem(gy, 2)
    dz, dx, dy, dc = lax.rem(step, 4), lax.rem(step // 4, 4), lax.rem(step // 16, 4), step // 64
    return (
        lax.rem(z + dz, 4) * 4 + lax.rem(x + dx, 4),
        lax.rem(y + dy, 4) * 2 + lax.rem(core + dc, 2),
    )


def split(value):
    high = value.astype(jnp.bfloat16)
    return high, (value - high.astype(jnp.float32)).astype(jnp.bfloat16)


def vertical_mix(levels, rows_x, coupling_t, source, mixed):
    padded = coupling_t.shape[0]
    stacked = jnp.concatenate(split(coupling_t[...]), axis=0)
    pad = jnp.zeros((padded - levels, 2 * LANES), jnp.float32)

    @pl.loop(0, rows_x // 2, unroll=2)
    def _(t):
        x = 2 * t
        pair = jnp.concatenate(
            [source[pl.ds(x, levels, stride=rows_x), :], source[pl.ds(x + 1, levels, stride=rows_x), :]], axis=1
        )
        high, low = split(jnp.concatenate([pair, pad], axis=0))
        both = jnp.dot(stacked, high, preferred_element_type=jnp.float32)
        out = both[:padded] + (
            both[padded:] + jnp.dot(stacked[:padded], low, preferred_element_type=jnp.float32)
        )
        mixed[pl.ds(x, levels, stride=rows_x), :] = out[:levels, :LANES]
        mixed[pl.ds(x + 1, levels, stride=rows_x), :] = out[:levels, LANES:]


def by_bank(levels, work):
    for bank, first in enumerate(range(0, levels, LANES)):
        count = min(LANES, levels - first)
        whole = count // WIDE

        @pl.loop(0, whole)
        def _(t):
            work(bank, first, t * WIDE, WIDE)

        if count % WIDE:
            work(bank, first, whole * WIDE, count % WIDE)


def spread(levels, rows_x, transport, mixed, out, row_edge, col_edge):
    row = lax.broadcasted_iota(jnp.int32, (rows_x, LANES), 0)
    lane = lax.broadcasted_iota(jnp.int32, (rows_x, LANES), 1)
    col_edge[...] = jnp.zeros_like(col_edge)

    def work(bank, first, spot, width):
        right_edge, left_edge = col_edge[0, bank], col_edge[1, bank]
        for i in range(width):
            at = spot + i
            l = first + at
            here = pl.ds(pl.multiple_of(l * rows_x, rows_x), rows_x)
            u = mixed[here, :]
            part = [transport[l, k].astype(jnp.float32) * u for k in range(5)]
            down = pltpu.roll(part[1], 1, 0)
            up = pltpu.roll(part[2], rows_x - 1, 0)
            right = pltpu.roll(part[3], 1, 1)
            left = pltpu.roll(part[4], LANES - 1, 1)
            row_edge[0, pl.ds(l, 1), :] = down[0:1]
            row_edge[1, pl.ds(l, 1), :] = up[rows_x - 1 : rows_x]
            mine = lane == at
            right_edge = jnp.where(mine, pltpu.roll(part[3], lax.rem(at + 1, LANES), 1), right_edge)
            left_edge = jnp.where(mine, pltpu.roll(part[4], at, 1), left_edge)
            total = part[0] + jnp.where(row == 0, 0.0, down) + jnp.where(row == rows_x - 1, 0.0, up)
            total = total + jnp.where(lane == 0, 0.0, right) + jnp.where(lane == LANES - 1, 0.0, left)
            out[here, :] = total
        col_edge[0, bank] = right_edge
        col_edge[1, bank] = left_edge

    by_bank(levels, work)


def add_edges(levels, rows_x, out, row_halo, col_halo, gx, gy, nx, ny):
    lane = lax.broadcasted_iota(jnp.int32, (rows_x, LANES), 1)
    first, last = pl.ds(0, levels, stride=rows_x), pl.ds(rows_x - 1, levels, stride=rows_x)
    out[first, :] = out[first, :] + jnp.where(gx > 0, row_halo[0, 0:levels, :], 0.0)
    out[last, :] = out[last, :] + jnp.where(gx < nx - 1, row_halo[1, 0:levels, :], 0.0)
    at_first = (lane == 0) & (gy > 0)
    at_last = (lane == LANES - 1) & (gy < ny - 1)

    def work(bank, start, spot, width):
        before_all, after_all = col_halo[0, bank], col_halo[1, bank]
        for i in range(width):
            at = spot + i
            here = pl.ds(pl.multiple_of((start + at) * rows_x, rows_x), rows_x)
            before = pltpu.roll(before_all, lax.rem(LANES - at, LANES), 1)
            after = pltpu.roll(after_all, LANES - 1 - at, 1)
            out[here, :] = out[here, :] + jnp.where(at_first, before, jnp.where(at_last, after, 0.0))

    by_bank(levels, work)


def build_table(levels, rows_x, field, table):
    eye = identity(LANES, jnp.bfloat16)

    @pl.loop(0, rows_x, unroll=4)
    def _(x):
        slab = field[pl.ds(x, levels, stride=rows_x), :]
        tail = jnp.concatenate([slab[MAIN:levels], jnp.zeros((2 * MAIN - levels, LANES), jnp.float32)], axis=0)
        base = pl.multiple_of(x * 2 * LANES, 2 * LANES)
        table[pl.ds(base, LANES, stride=2), :] = dot_nt(eye, slab[:MAIN].astype(jnp.bfloat16))
        table[pl.ds(base + 1, LANES, stride=2), :] = dot_nt(eye, tail.astype(jnp.bfloat16))


def exchange_kernel(
    levels,
    columns,
    gradient,
    coupling_t,
    transport,
    field,
    received,
    mixed,
    row_edge,
    col_edge,
    row_halo,
    col_halo,
    table,
    ga,
    gb,
    outgoing,
    edge_send,
    edge_recv,
    send_sem,
    recv_sem,
    own_sem,
):
    gx, gy = lax.axis_index("gx"), lax.axis_index("gy")
    nx, ny = lax.axis_size("gx"), lax.axis_size("gy")
    me = gx * ny + gy
    ranks = received.shape[0]
    barrier = pltpu.get_barrier_semaphore()

    @pl.loop(1, ranks)
    def _(k):
        pl.semaphore_signal(barrier, inc=1, device_id=peer(k), device_id_type=MESH)

    rows_x = field.shape[0] // levels
    sides = (
        (row_edge, row_halo, 0, (lax.rem(gx + 1, nx), gy)),
        (row_edge, row_halo, 1, (lax.rem(gx + nx - 1, nx), gy)),
        (col_edge, col_halo, 0, (gx, lax.rem(gy + 1, ny))),
        (col_edge, col_halo, 1, (gx, lax.rem(gy + ny - 1, ny))),
    )
    for step in range(STEPS):
        vertical_mix(levels, rows_x, coupling_t, gradient if step == 0 else field, mixed)
        spread(levels, rows_x, transport, mixed, field, row_edge.at[step], col_edge.at[step])
        if step == 0:
            pl.semaphore_wait(barrier, ranks - 1)
        copies = [
            pltpu.make_async_remote_copy(
                src_ref=edge.at[step, side],
                dst_ref=halo.at[step, side],
                send_sem=edge_send.at[step, i],
                recv_sem=edge_recv.at[step, i],
                device_id=device,
                device_id_type=MESH,
            )
            for i, (edge, halo, side, device) in enumerate(sides)
        ]
        for copy in copies:
            copy.start()
        for copy in copies:
            copy.wait()
        add_edges(levels, rows_x, field, row_halo.at[step], col_halo.at[step], gx, gy, nx, ny)

    build_table(levels, rows_x, field, table)
    pick = identity(TAIL, jnp.bfloat16)

    def step_at(k):
        return lax.rem((k + 1) * STRIDE, ranks)

    def owner_at(k):
        tx, ty = peer(step_at(k))
        return tx * ny + ty

    def copy_for(k):
        step = step_at(k)
        tx, ty = peer(step)
        return pltpu.make_async_remote_copy(
            src_ref=outgoing.at[tx * ny + ty],
            dst_ref=received.at[me],
            send_sem=send_sem.at[step],
            recv_sem=recv_sem.at[step],
            device_id=(tx, ty),
            device_id_type=MESH,
        )

    def gather(k, rows, first, count):
        base = owner_at(k) * LANES
        for i in range(first, first + count, GROUP):
            got = [table[pl.ds(columns[base + i + j], 2), :] for j in range(GROUP)]
            for j in range(GROUP):
                rows[pl.ds((i + j) * 2, 2), :] = got[j]

    def pack(k, rows, next_k, next_rows):
        owner = owner_at(k)
        main = rows[pl.ds(0, LANES, stride=2), :].astype(jnp.bfloat16)
        tail = rows[pl.ds(1, LANES, stride=2), :].astype(jnp.bfloat16)
        packed = dot_nt(pick, tail)
        gather(next_k, next_rows, 0, LANES)
        outgoing[owner, 0:MAIN, :] = main
        outgoing[owner, MAIN:BLOCK, :] = packed.astype(jnp.bfloat16)

    gather(0, ga, 0, LANES)

    @pl.loop(0, ranks // 2)
    def _(t):
        k = t * 2
        pack(k, ga, k + 1, gb)
        copy_for(k).start()
        pack(k + 1, gb, jnp.minimum(k + 2, ranks - 1), ga)

        @pl.when(k + 1 < ranks - 1)
        def _():
            copy_for(k + 1).start()

    own = pltpu.make_async_copy(outgoing.at[me], received.at[me], own_sem)
    own.start()

    @pl.loop(0, ranks - 1)
    def _(k):
        copy_for(k).wait()

    own.wait()


def exchange(columns, gradient, coupling, transport, ranks):
    levels, rows_x, lanes = gradient.shape
    flat = gradient.reshape(levels * rows_x, lanes)
    padded = -(-levels // TAIL) * TAIL
    coupling_t = jnp.pad(coupling.T, ((0, padded - levels), (0, padded - levels)))
    block = jax.ShapeDtypeStruct((ranks, BLOCK, LANES), jnp.bfloat16)
    row_edges = pltpu.VMEM((STEPS, 2, padded, LANES), jnp.float32)
    col_edges = pltpu.VMEM((STEPS, 2, 2, rows_x, LANES), jnp.float32)

    def kernel(*refs):
        exchange_kernel(levels, *refs)

    field, received = pl.pallas_call(
        kernel,
        out_shape=(jax.ShapeDtypeStruct(flat.shape, jnp.float32), block),
        in_specs=[SMEM, VMEM, VMEM, VMEM],
        out_specs=(VMEM, VMEM),
        scratch_shapes=[
            pltpu.VMEM(flat.shape, jnp.float32),
            row_edges,
            col_edges,
            row_edges,
            col_edges,
            pltpu.VMEM((rows_x * lanes * 2, LANES), jnp.float32),
            pltpu.VMEM((2 * LANES, LANES), jnp.float32),
            pltpu.VMEM((2 * LANES, LANES), jnp.float32),
            pltpu.VMEM(block.shape, block.dtype),
            pltpu.SemaphoreType.DMA((STEPS, 4)),
            pltpu.SemaphoreType.DMA((STEPS, 4)),
            pltpu.SemaphoreType.DMA((ranks,)),
            pltpu.SemaphoreType.DMA((ranks,)),
            pltpu.SemaphoreType.DMA,
        ],
        compiler_params=pltpu.CompilerParams(collective_id=1, has_side_effects=True, vmem_limit_bytes=48 * MIB),
        name="exchange",
    )(columns, flat, coupling_t, transport)
    return field.reshape(gradient.shape), received


def impact_kernel(slots, valid, received, jac, weight, innovation, inst, impact, part, table, ga, gb):
    levels, holders, chunks = jac.shape[0], received.shape[0], impact.shape[0]
    eye = identity(LANES, jnp.int32) == 1
    spread_tail = identity(TAIL, jnp.bfloat16)

    @pl.loop(0, holders, unroll=8)
    def _(h):
        base = pl.multiple_of(h * 2 * LANES, 2 * LANES)
        table[pl.ds(base, LANES, stride=2), :] = received[h, 0:MAIN, :].astype(jnp.float32)
        table[pl.ds(base + 1, LANES, stride=2), :] = lax.dot_general(
            received[h, MAIN:BLOCK, :], spread_tail, (((0,), (0,)), ((), ())), preferred_element_type=jnp.float32
        )

    part[...] = jnp.zeros_like(part)
    lane = lax.broadcasted_iota(jnp.int32, (1, LANES), 1)
    points = 4
    rows_per = points * LANES

    def gather(j, rows, first, count):
        for i in range(first, first + count, GROUP):
            got = [table[pl.ds(slots[j * rows_per + i + k], 2), :] for k in range(GROUP)]
            for k in range(GROUP):
                rows[pl.ds((i + k) * 2, 2), :] = got[k]

    def work(j, rows, next_j, next_rows):
        col = pl.multiple_of(j * LANES, LANES)
        tail = jnp.concatenate(
            [
                jac[MAIN:levels, pl.ds(col, LANES)].astype(jnp.float32),
                jnp.zeros((BLOCK - levels, LANES), jnp.float32),
            ],
            axis=0,
        ).astype(jnp.bfloat16)
        profile = jnp.concatenate(
            [jac[0:MAIN, pl.ds(col, LANES)], tail, jnp.zeros((2 * MAIN - BLOCK, LANES), jnp.bfloat16)], axis=0
        )
        total = jnp.zeros((1, LANES), jnp.float32)
        for c in range(points):
            main = rows[pl.ds(c * 2 * LANES, LANES, stride=2), :].astype(jnp.bfloat16)
            rest = rows[pl.ds(c * 2 * LANES + 1, LANES, stride=2), :].astype(jnp.bfloat16)
            products = jnp.dot(
                jnp.concatenate([main, rest], axis=1), profile, preferred_element_type=jnp.float32
            )
            gather(next_j, next_rows, c * LANES, LANES // 2)
            diagonal = jnp.sum(jnp.where(eye, products, 0.0), axis=0, keepdims=True)
            total = total + diagonal * weight[c : c + 1, pl.ds(col, LANES)]
            gather(next_j, next_rows, c * LANES + LANES // 2, LANES // 2)
        value = innovation[pl.ds(j, 1), :] * total
        value = jnp.where(lane + j * LANES < valid[0], value, 0.0)
        impact[pl.ds(j, 1), :] = value
        same = lax.broadcasted_iota(jnp.int32, (NI, LANES), 0) == inst[pl.ds(j, 1), :]
        part[...] += jnp.where(same, value, 0.0)

    gather(0, ga, 0, rows_per)

    @pl.loop(0, chunks // 2)
    def _(t):
        j = t * 2
        work(j, ga, j + 1, gb)
        work(j + 1, gb, jnp.minimum(j + 2, chunks - 1), ga)


def impacts(slots, valid, received, jac, weight, innovation, inst):
    count, holders = innovation.shape[0], received.shape[0]
    chunks = count // LANES
    slots = (slots * 2).reshape(4, chunks, LANES).transpose(1, 0, 2).reshape(4 * count)
    impact, part = pl.pallas_call(
        impact_kernel,
        out_shape=(
            jax.ShapeDtypeStruct((chunks, LANES), jnp.float32),
            jax.ShapeDtypeStruct((NI, LANES), jnp.float32),
        ),
        in_specs=[SMEM, SMEM] + [VMEM] * 5,
        out_specs=(VMEM, VMEM),
        scratch_shapes=[
            pltpu.VMEM((holders * 2 * LANES, LANES), jnp.float32),
            pltpu.VMEM((4 * 2 * LANES, LANES), jnp.float32),
            pltpu.VMEM((4 * 2 * LANES, LANES), jnp.float32),
        ],
        compiler_params=pltpu.CompilerParams(vmem_limit_bytes=48 * MIB),
        name="impacts",
    )(slots, valid, received, jac, weight, innovation.reshape(chunks, LANES), inst.reshape(chunks, LANES))
    return impact.reshape(count), part


def total_kernel(part, total, first, second, send_sem, recv_sem):
    gx, gy = lax.axis_index("gx"), lax.axis_index("gy")
    nx, ny = first.shape[0], second.shape[0]
    barrier = pltpu.get_barrier_semaphore()
    for k in range(1, ny):
        pl.semaphore_signal(barrier, inc=1, device_id=(gx, lax.rem(gy + k, ny)), device_id_type=MESH)
    for k in range(1, nx):
        pl.semaphore_signal(barrier, inc=1, device_id=(lax.rem(gx + k, nx), gy), device_id_type=MESH)
    rows = lax.dot_general(
        jnp.ones((8, LANES), jnp.float32),
        part[...],
        (((1,), (1,)), ((), ())),
        precision=lax.Precision.HIGHEST,
        preferred_element_type=jnp.float32,
    )
    own = jnp.concatenate([rows, jnp.zeros((8, LANES - NI), jnp.float32)], axis=1)
    pl.semaphore_wait(barrier, nx + ny - 2)

    def share(value, slots, size, me, coords, base):
        slots[me] = value
        copies = [
            pltpu.make_async_remote_copy(
                src_ref=slots.at[me],
                dst_ref=slots.at[me],
                send_sem=send_sem.at[base + k],
                recv_sem=recv_sem.at[base + k],
                device_id=coords(lax.rem(me + k, size)),
                device_id_type=MESH,
            )
            for k in range(1, size)
        ]
        for copy in copies:
            copy.start()
        for copy in copies:
            copy.wait()
        out = slots[0]
        for k in range(1, size):
            out = out + slots[k]
        return out

    across = share(own, second, ny, gy, lambda i: (gx, i), 0)
    total[...] = share(across, first, nx, gx, lambda i: (i, gy), ny)


def instrument_totals(part, nx, ny):
    total = pl.pallas_call(
        total_kernel,
        out_shape=jax.ShapeDtypeStruct((8, LANES), jnp.float32),
        in_specs=[VMEM],
        out_specs=VMEM,
        scratch_shapes=[
            pltpu.VMEM((nx, 8, LANES), jnp.float32),
            pltpu.VMEM((ny, 8, LANES), jnp.float32),
            pltpu.SemaphoreType.DMA((nx + ny,)),
            pltpu.SemaphoreType.DMA((nx + ny,)),
        ],
        compiler_params=pltpu.CompilerParams(collective_id=2, has_side_effects=True),
        name="totals",
    )(part)
    return total[0, :NI]


def body(
    gradient,
    coupling,
    transport,
    obs_jacobian,
    send_cols,
    obs_slots,
    obs_weight,
    obs_inst,
    innovation,
    valid_count,
):
    nx, ny = lax.axis_size("gx"), lax.axis_size("gy")
    columns = jnp.maximum(send_cols[0], 0) * 2
    sensitivity, received = exchange(columns, gradient, coupling, transport, nx * ny)
    impact, part = impacts(
        obs_slots, valid_count, received, obs_jacobian, obs_weight, innovation, obs_inst
    )
    return (sensitivity, impact, instrument_totals(part, nx, ny))


def solution(mesh):
    placed = (
        P(None, "gx", "gy"),
        P(),
        P(None, None, "gx", "gy"),
        P(None, ("gx", "gy")),
        P(("gx", "gy"), None),
        P(None, ("gx", "gy")),
        P(None, ("gx", "gy")),
        P(("gx", "gy")),
        P(("gx", "gy")),
        P(("gx", "gy")),
    )
    return jax.shard_map(
        body,
        mesh=mesh,
        in_specs=placed,
        out_specs=(P(None, "gx", "gy"), P(("gx", "gy")), P()),
        check_vma=False,
    )
```

```python
import jax
import jax.numpy as jnp
from jax import lax
from jax.experimental import pallas as pl
from jax.experimental.pallas import tpu as pltpu
from jax.sharding import PartitionSpec as P

NI = 32
STEPS = 2
LANES = 128
MAIN = 128
TAIL = 16
BLOCK = MAIN + TAIL
GROUP = 8
WIDE = 8
MIX_UNROLL = 2
FRONT = 8
POINTS = 4
EXPAND = 4
STRIDE = 37
MESH = pl.DeviceIdType.MESH
VMEM = pl.BlockSpec(memory_space=pltpu.VMEM)
SMEM = pl.BlockSpec(memory_space=pltpu.SMEM)
ANY = pl.BlockSpec(memory_space=pl.ANY)
MIB = 1024 * 1024


def identity(rows, dtype):
    row = lax.broadcasted_iota(jnp.int32, (rows, LANES), 0)
    col = lax.broadcasted_iota(jnp.int32, (rows, LANES), 1)
    return (row == col).astype(dtype)


def dot_nt(a, b):
    return lax.dot_general(a, b, (((1,), (1,)), ((), ())), preferred_element_type=jnp.float32)


def moved(step, sign):
    gx, gy = lax.axis_index("gx"), lax.axis_index("gy")
    z, x, y, core = gx // 4, lax.rem(gx, 4), gy // 2, lax.rem(gy, 2)
    dz, dx, dy, dc = lax.rem(step, 4), lax.rem(step // 4, 4), lax.rem(step // 16, 4), step // 64
    if sign < 0:
        dz, dx, dy = 4 - dz, 4 - dx, 4 - dy
    return (
        lax.rem(z + dz, 4) * 4 + lax.rem(x + dx, 4),
        lax.rem(y + dy, 4) * 2 + lax.rem(core + dc, 2),
    )


def peer(step):
    return moved(step, 1)


def split(value):
    high = value.astype(jnp.bfloat16)
    return high, (value - high.astype(jnp.float32)).astype(jnp.bfloat16)


def product(parts_a, parts_b):
    high_a, low_a = parts_a
    high_b, low_b = parts_b
    one = jnp.dot(high_a, high_b, preferred_element_type=jnp.float32)
    two = jnp.dot(low_a, high_b, preferred_element_type=jnp.float32)
    return one + (two + jnp.dot(high_a, low_b, preferred_element_type=jnp.float32))


def vertical_mix(levels, rows_x, coupling_t, source, mixed):
    padded = coupling_t.shape[1]
    stacked = coupling_t[...].reshape(2 * padded, padded)
    pad = jnp.zeros((padded - levels, 2 * LANES), jnp.float32)

    @pl.loop(0, rows_x // 2, unroll=MIX_UNROLL)
    def _(t):
        x = 2 * t
        pair = jnp.concatenate(
            [source[pl.ds(x, levels, stride=rows_x), :], source[pl.ds(x + 1, levels, stride=rows_x), :]], axis=1
        )
        high, low = split(jnp.concatenate([pair, pad], axis=0))
        both = jnp.dot(stacked, high, preferred_element_type=jnp.float32)
        out = both[:padded] + (
            both[padded:] + jnp.dot(stacked[:padded], low, preferred_element_type=jnp.float32)
        )
        mixed[pl.ds(x, levels, stride=rows_x), :] = out[:levels, :LANES]
        mixed[pl.ds(x + 1, levels, stride=rows_x), :] = out[:levels, LANES:]


def by_bank(levels, work):
    for bank, first in enumerate(range(0, levels, LANES)):
        count = min(LANES, levels - first)
        whole = count // WIDE

        @pl.loop(0, whole)
        def _(t):
            work(bank, first, t * WIDE, WIDE)

        if count % WIDE:
            work(bank, first, whole * WIDE, count % WIDE)


def at_edges(lane, first, last):
    return jnp.where(lane == 0, first, jnp.where(lane == LANES - 1, last, 0.0))


def spread(levels, rows_x, transport, mixed, out, row_edge, col_edge, col_mixed, col_own):
    row = lax.broadcasted_iota(jnp.int32, (rows_x, LANES), 0)
    lane = lax.broadcasted_iota(jnp.int32, (rows_x, LANES), 1)

    def work(bank, first, spot, width):
        right_edge, left_edge = col_edge[0, bank], col_edge[1, bank]
        if col_mixed is not None:
            before_all, after_all = col_mixed[0, bank], col_mixed[1, bank]
            first_own, last_own = col_own[0, bank], col_own[1, bank]
        for i in range(width):
            at = spot + i
            l = first + at
            here = pl.ds(pl.multiple_of(l * rows_x, rows_x), rows_x)
            u = mixed[here, :]
            if col_mixed is not None:
                before = pltpu.roll(before_all, lax.rem(LANES - at, LANES), 1)
                after = pltpu.roll(after_all, LANES - 1 - at, 1)
                u = u + at_edges(lane, before, after)
            part = [transport[l, k].astype(jnp.float32) * u for k in range(5)]
            down = pltpu.roll(part[1], 1, 0)
            up = pltpu.roll(part[2], rows_x - 1, 0)
            right = pltpu.roll(part[3], 1, 1)
            left = pltpu.roll(part[4], LANES - 1, 1)
            row_edge[0, pl.ds(l, 1), :] = down[0:1]
            row_edge[1, pl.ds(l, 1), :] = up[rows_x - 1 : rows_x]
            mine = lane == at
            right_edge = jnp.where(mine, pltpu.roll(part[3], lax.rem(at + 1, LANES), 1), right_edge)
            left_edge = jnp.where(mine, pltpu.roll(part[4], at, 1), left_edge)
            total = part[0] + jnp.where(row == 0, 0.0, down) + jnp.where(row == rows_x - 1, 0.0, up)
            total = total + jnp.where(lane == 0, 0.0, right) + jnp.where(lane == LANES - 1, 0.0, left)
            out[here, :] = total
            if col_mixed is not None:
                first_own = jnp.where(mine, pltpu.roll(total, at, 1), first_own)
                last_own = jnp.where(mine, pltpu.roll(total, lax.rem(at + 1, LANES), 1), last_own)
        col_edge[0, bank] = right_edge
        col_edge[1, bank] = left_edge
        if col_mixed is not None:
            col_own[0, bank] = first_own
            col_own[1, bank] = last_own

    by_bank(levels, work)


def add_columns(levels, rows_x, out, col_halo):
    lane = lax.broadcasted_iota(jnp.int32, (rows_x, LANES), 1)

    def work(bank, start, spot, width):
        before_all, after_all = col_halo[0, bank], col_halo[1, bank]
        for i in range(width):
            at = spot + i
            here = pl.ds(pl.multiple_of((start + at) * rows_x, rows_x), rows_x)
            before = pltpu.roll(before_all, lax.rem(LANES - at, LANES), 1)
            after = pltpu.roll(after_all, LANES - 1 - at, 1)
            out[here, :] = out[here, :] + at_edges(lane, before, after)

    by_bank(levels, work)


def table_rows(levels, rows_x, field, table, x):
    eye = identity(LANES, jnp.bfloat16)
    slab = field[pl.ds(x, levels, stride=rows_x), :]
    tail = jnp.concatenate([slab[MAIN:levels], jnp.zeros((2 * MAIN - levels, LANES), jnp.float32)], axis=0)
    base = FRONT + x * 2 * LANES
    table[pl.ds(base, LANES, stride=2), :] = dot_nt(eye, slab[:MAIN].astype(jnp.bfloat16))
    table[pl.ds(base + 1, LANES, stride=2), :] = dot_nt(eye, tail.astype(jnp.bfloat16))


def whole_kernel(
    columns,
    valid,
    gradient,
    coupling,
    transport_in,
    jac_in,
    slots_in,
    weight,
    innovation,
    inst,
    field,
    impact,
    total,
    transport,
    jac,
    slots_v,
    slots,
    square,
    coupling_t,
    mixed,
    row_edge,
    col_edge,
    row_halo,
    col_halo,
    col_mixed,
    col_own,
    table,
    ga,
    gb,
    outgoing,
    received,
    profiles,
    oa,
    ob,
    part,
    shares,
    edge_send,
    edge_recv,
    send_sem,
    recv_sem,
    share_send,
    share_recv,
    local_sem,
):
    gx, gy = lax.axis_index("gx"), lax.axis_index("gy")
    nx, ny = lax.axis_size("gx"), lax.axis_size("gy")
    me = gx * ny + gy
    ranks = received.shape[0]
    levels = coupling.shape[0]
    rows_x = field.shape[0] // levels
    padded = coupling_t.shape[1]
    chunks = impact.shape[0]
    barrier = pltpu.get_barrier_semaphore()

    load_transport = pltpu.make_async_copy(transport_in, transport, local_sem.at[0])
    load_transport.start()
    load_jac = pltpu.make_async_copy(jac_in, jac, local_sem.at[1])
    load_jac.start()

    @pl.loop(1, ranks)
    def _(k):
        pl.semaphore_signal(barrier, inc=1, device_id=peer(k), device_id_type=MESH)

    square[...] = jnp.zeros_like(square)
    square[0:levels, 0:levels] = coupling[...]
    coupling_parts = split(square[...])
    side = square.shape[0]
    wide_eye = (
        lax.broadcasted_iota(jnp.int32, (padded, side), 0) == lax.broadcasted_iota(jnp.int32, (padded, side), 1)
    ).astype(jnp.bfloat16)
    for i in range(2):
        coupling_t[i] = dot_nt(wide_eye, coupling_parts[i])[:, :padded].astype(jnp.bfloat16)
    col_edge[...] = jnp.zeros_like(col_edge)
    col_own[...] = jnp.zeros_like(col_own)
    table[0:FRONT, :] = jnp.zeros((FRONT, LANES), jnp.float32)

    sides = (
        (row_edge, row_halo, 0, (lax.rem(gx + 1, nx), gy)),
        (row_edge, row_halo, 1, (lax.rem(gx + nx - 1, nx), gy)),
        (col_edge, col_halo, 0, (gx, lax.rem(gy + 1, ny))),
        (col_edge, col_halo, 1, (gx, lax.rem(gy + ny - 1, ny))),
    )
    inside = (gx > 0, gx < nx - 1, gy > 0, gy < ny - 1)
    ends = (pl.ds(0, levels, stride=rows_x), pl.ds(rows_x - 1, levels, stride=rows_x))

    def edge_copies(step):
        return [
            pltpu.make_async_remote_copy(
                src_ref=edge.at[step, which],
                dst_ref=halo.at[step, which],
                send_sem=edge_send.at[step, i],
                recv_sem=edge_recv.at[step, i],
                device_id=device,
                device_id_type=MESH,
            )
            for i, (edge, halo, which, device) in enumerate(sides)
        ]

    def row_values(step, which):
        return jnp.where(inside[which], row_halo[step, which, 0:levels, :], 0.0)

    vertical_mix(levels, rows_x, coupling_t, gradient, mixed)
    load_transport.wait()
    spread(levels, rows_x, transport, mixed, field, row_edge.at[0], col_edge.at[0], None, None)
    pl.semaphore_wait(barrier, ranks - 1)
    copies = edge_copies(0)
    for copy in copies:
        copy.start()
    vertical_mix(levels, rows_x, coupling_t, field, mixed)
    for copy in copies:
        copy.wait()
    both = jnp.concatenate([row_values(0, 0), row_values(0, 1)], axis=1)
    both = jnp.concatenate([both, jnp.zeros((padded - levels, 2 * LANES), jnp.float32)], axis=0)
    added = product((coupling_t[0], coupling_t[1]), split(both))
    for which in range(2):
        mixed[ends[which], :] = mixed[ends[which], :] + added[:levels, which * LANES : (which + 1) * LANES]
    strips = jnp.concatenate(
        [
            jnp.where(inside[2 + which], jnp.concatenate([col_halo[0, which, 0], col_halo[0, which, 1]], axis=1), 0.0)
            for which in range(2)
        ],
        axis=0,
    )
    strips = product(split(strips), coupling_parts)
    for which in range(2):
        for bank in range(2):
            col_mixed[which, bank] = strips[
                which * rows_x : (which + 1) * rows_x, bank * LANES : (bank + 1) * LANES
            ]

    spread(levels, rows_x, transport, mixed, field, row_edge.at[1], col_edge.at[1], col_mixed, col_own)
    copies = edge_copies(1)
    for copy in copies:
        copy.start()

    @pl.loop(0, (rows_x - 2) // 3)
    def _(t):
        for i in range(3):
            table_rows(levels, rows_x, field, table, 1 + t * 3 + i)

    slots_v[...] = slots_in[...] * 2
    load_slots = pltpu.make_async_copy(slots_v, slots, local_sem.at[2])
    load_slots.start()
    for copy in copies:
        copy.wait()
    corners = (
        (lax.broadcasted_iota(jnp.int32, (8, LANES), 0) * (LANES - 1) == lax.broadcasted_iota(jnp.int32, (8, LANES), 1))
        & (lax.broadcasted_iota(jnp.int32, (8, LANES), 0) < 2)
    ).astype(jnp.float32)
    for which in range(2):
        x = which * (rows_x - 1)
        halo = row_values(1, which)
        field[ends[which], :] = field[ends[which], :] + halo
        table_rows(levels, rows_x, field, table, x)
        halo = jnp.concatenate([halo, jnp.zeros((side - levels, LANES), jnp.float32)], axis=0)
        crossing = lax.dot_general(
            corners,
            halo,
            (((1,), (1,)), ((), ())),
            precision=lax.Precision.HIGHEST,
            preferred_element_type=jnp.float32,
        )
        for end in range(2):
            for bank in range(2):
                spot = col_own.at[end, bank]
                spot[x : x + 1, :] = spot[x : x + 1, :] + crossing[end : end + 1, bank * LANES : (bank + 1) * LANES]
    for end in range(2):
        for bank in range(2):
            strip = jnp.where(inside[2 + end], col_halo[1, end, bank], 0.0)
            col_mixed[end, bank] = strip
            table[pl.ds(FRONT + end * 2 * (LANES - 1) + bank, rows_x, stride=2 * LANES), :] = col_own[end, bank] + strip

    pick = identity(TAIL, jnp.bfloat16)

    def step_at(k):
        return lax.rem((k + 1) * STRIDE, ranks)

    def owner_at(k):
        tx, ty = peer(step_at(k))
        return tx * ny + ty

    def copy_for(k):
        step = step_at(k)
        tx, ty = peer(step)
        return pltpu.make_async_remote_copy(
            src_ref=outgoing.at[tx * ny + ty],
            dst_ref=received.at[me],
            send_sem=send_sem.at[step],
            recv_sem=recv_sem.at[step],
            device_id=(tx, ty),
            device_id_type=MESH,
        )

    def gather(k, rows):
        base = owner_at(k) * LANES
        for i in range(0, LANES, GROUP):
            got = [table[pl.ds(columns[base + i + j] * 2 + FRONT, 2), :] for j in range(GROUP)]
            for j in range(GROUP):
                rows[pl.ds((i + j) * 2, 2), :] = got[j]

    def pack(k, rows, next_k, next_rows):
        owner = owner_at(k)
        main = rows[pl.ds(0, LANES, stride=2), :].astype(jnp.bfloat16)
        tail = rows[pl.ds(1, LANES, stride=2), :].astype(jnp.bfloat16)
        packed = dot_nt(pick, tail)
        gather(next_k, next_rows)
        outgoing[owner, 0:MAIN, :] = main
        outgoing[owner, MAIN:BLOCK, :] = packed.astype(jnp.bfloat16)

    gather(0, ga)

    @pl.loop(0, ranks // 2)
    def _(t):
        k = t * 2
        pack(k, ga, k + 1, gb)
        copy_for(k).start()
        pack(k + 1, gb, jnp.minimum(k + 2, ranks - 1), ga)

        @pl.when(k + 1 < ranks - 1)
        def _():
            copy_for(k + 1).start()

    own = pltpu.make_async_copy(outgoing.at[me], received.at[me], local_sem.at[3])
    own.start()

    add_columns(levels, rows_x, field, col_mixed)
    part[...] = jnp.zeros_like(part)
    load_jac.wait()
    load_slots.wait()
    own.wait()

    spread_tail = identity(TAIL, jnp.bfloat16)

    def expand(h):
        base = pl.multiple_of(h * 2 * LANES, 2 * LANES)
        profiles[pl.ds(base, LANES, stride=2), :] = received[h, 0:MAIN, :].astype(jnp.float32)
        profiles[pl.ds(base + 1, LANES, stride=2), :] = lax.dot_general(
            received[h, MAIN:BLOCK, :], spread_tail, (((0,), (0,)), ((), ())), preferred_element_type=jnp.float32
        )

    def holder_at(k):
        hx, hy = moved(step_at(k), -1)
        return hx * ny + hy

    @pl.loop(0, ranks // EXPAND)
    def _(t):
        for i in range(EXPAND):
            k = t * EXPAND + i

            @pl.when(k < ranks - 1)
            def _():
                copy_for(k).wait_recv()

        for i in range(EXPAND):
            expand(holder_at(t * EXPAND + i))

    eye = identity(LANES, jnp.int32) == 1
    lane = lax.broadcasted_iota(jnp.int32, (1, LANES), 1)

    def fetch(j, rows, c, first, count):
        line = j * POINTS + c
        for i in range(first, first + count, GROUP):
            got = [profiles[pl.ds(slots[line, i + k], 2), :] for k in range(GROUP)]
            for k in range(GROUP):
                rows[pl.ds((c * LANES + i + k) * 2, 2), :] = got[k]

    def work(j, rows, next_j, next_rows):
        col = pl.multiple_of(j * LANES, LANES)
        tail = jnp.concatenate(
            [
                jac[MAIN:levels, pl.ds(col, LANES)].astype(jnp.float32),
                jnp.zeros((BLOCK - levels, LANES), jnp.float32),
            ],
            axis=0,
        ).astype(jnp.bfloat16)
        profile = jnp.concatenate(
            [jac[0:MAIN, pl.ds(col, LANES)], tail, jnp.zeros((2 * MAIN - BLOCK, LANES), jnp.bfloat16)], axis=0
        )
        value = jnp.zeros((1, LANES), jnp.float32)
        for c in range(POINTS):
            main = rows[pl.ds(c * 2 * LANES, LANES, stride=2), :].astype(jnp.bfloat16)
            rest = rows[pl.ds(c * 2 * LANES + 1, LANES, stride=2), :].astype(jnp.bfloat16)
            products = jnp.dot(
                jnp.concatenate([main, rest], axis=1), profile, preferred_element_type=jnp.float32
            )
            fetch(next_j, next_rows, c, 0, LANES // 2)
            diagonal = jnp.sum(jnp.where(eye, products, 0.0), axis=0, keepdims=True)
            value = value + diagonal * weight[c : c + 1, pl.ds(col, LANES)]
            fetch(next_j, next_rows, c, LANES // 2, LANES // 2)
        value = innovation[pl.ds(j, 1), :] * value
        value = jnp.where(lane + j * LANES < valid[0], value, 0.0)
        impact[pl.ds(j, 1), :] = value
        same = lax.broadcasted_iota(jnp.int32, (NI, LANES), 0) == inst[pl.ds(j, 1), :]
        part[...] += jnp.where(same, value, 0.0)

    for c in range(POINTS):
        fetch(0, oa, c, 0, LANES)

    @pl.loop(0, chunks // 2)
    def _(t):
        j = t * 2
        work(j, oa, j + 1, ob)
        work(j + 1, ob, jnp.minimum(j + 2, chunks - 1), oa)

    rows = lax.dot_general(
        jnp.ones((8, LANES), jnp.float32),
        part[...],
        (((1,), (1,)), ((), ())),
        precision=lax.Precision.HIGHEST,
        preferred_element_type=jnp.float32,
    )
    shares[me] = jnp.concatenate([rows, jnp.zeros((8, LANES - NI), jnp.float32)], axis=1)

    def share(k):
        return pltpu.make_async_remote_copy(
            src_ref=shares.at[me],
            dst_ref=shares.at[me],
            send_sem=share_send.at[k],
            recv_sem=share_recv.at[k],
            device_id=peer(k),
            device_id_type=MESH,
        )

    @pl.loop(1, ranks)
    def _(k):
        share(k).start()

    @pl.loop(0, ranks - 1)
    def _(k):
        copy_for(k).wait_send()

    @pl.loop(1, ranks)
    def _(k):
        share(k).wait()

    total[...] = jnp.sum(shares[...], axis=0)


def run(columns, valid, gradient, coupling, transport, jac, slots, weight, innovation, inst, ranks):
    levels, rows_x, lanes = gradient.shape
    count = innovation.shape[0]
    chunks = count // LANES
    flat = gradient.reshape(levels * rows_x, lanes)
    padded = -(-levels // TAIL) * TAIL
    slots = slots.reshape(POINTS, chunks, LANES).transpose(1, 0, 2).reshape(chunks * POINTS, LANES)
    f32, bf16 = jnp.float32, jnp.bfloat16
    row_edges = pltpu.VMEM((STEPS, 2, padded, LANES), f32)
    col_edges = pltpu.VMEM((STEPS, 2, 2, rows_x, LANES), f32)
    block = pltpu.VMEM((ranks, BLOCK, LANES), bf16)
    field, impact, total = pl.pallas_call(
        whole_kernel,
        out_shape=(
            jax.ShapeDtypeStruct(flat.shape, f32),
            jax.ShapeDtypeStruct((chunks, LANES), f32),
            jax.ShapeDtypeStruct((8, LANES), f32),
        ),
        in_specs=[SMEM, SMEM, VMEM, VMEM, ANY, ANY, VMEM, VMEM, VMEM, VMEM],
        out_specs=(VMEM, VMEM, VMEM),
        scratch_shapes=[
            pltpu.VMEM(transport.shape, bf16),
            pltpu.VMEM(jac.shape, bf16),
            pltpu.VMEM(slots.shape, jnp.int32),
            pltpu.SMEM(slots.shape, jnp.int32),
            pltpu.VMEM((2 * MAIN, 2 * MAIN), f32),
            pltpu.VMEM((2, padded, padded), bf16),
            pltpu.VMEM(flat.shape, f32),
            row_edges,
            col_edges,
            row_edges,
            col_edges,
            pltpu.VMEM((2, 2, rows_x, LANES), f32),
            pltpu.VMEM((2, 2, rows_x, LANES), f32),
            pltpu.VMEM((FRONT + rows_x * lanes * 2, LANES), f32),
            pltpu.VMEM((2 * LANES, LANES), f32),
            pltpu.VMEM((2 * LANES, LANES), f32),
            block,
            block,
            pltpu.VMEM((ranks * 2 * LANES, LANES), f32),
            pltpu.VMEM((POINTS * 2 * LANES, LANES), f32),
            pltpu.VMEM((POINTS * 2 * LANES, LANES), f32),
            pltpu.VMEM((NI, LANES), f32),
            pltpu.VMEM((ranks, 8, LANES), f32),
            pltpu.SemaphoreType.DMA((STEPS, 4)),
            pltpu.SemaphoreType.DMA((STEPS, 4)),
            pltpu.SemaphoreType.DMA((ranks,)),
            pltpu.SemaphoreType.DMA((ranks,)),
            pltpu.SemaphoreType.DMA((ranks,)),
            pltpu.SemaphoreType.DMA((ranks,)),
            pltpu.SemaphoreType.DMA((4,)),
        ],
        compiler_params=pltpu.CompilerParams(collective_id=1, has_side_effects=True, vmem_limit_bytes=58 * MIB),
        name="whole",
    )(
        columns,
        valid,
        flat,
        coupling,
        transport,
        jac,
        slots,
        weight,
        innovation.reshape(chunks, LANES),
        inst.reshape(chunks, LANES),
    )
    return field.reshape(gradient.shape), impact.reshape(count), total[0, :NI]


def body(
    gradient,
    coupling,
    transport,
    obs_jacobian,
    send_cols,
    obs_slots,
    obs_weight,
    obs_inst,
    innovation,
    valid_count,
):
    ranks = lax.axis_size("gx") * lax.axis_size("gy")
    return run(
        send_cols[0],
        valid_count,
        gradient,
        coupling,
        transport,
        obs_jacobian,
        obs_slots,
        obs_weight,
        innovation,
        obs_inst,
        ranks,
    )


def solution(mesh):
    placed = (
        P(None, "gx", "gy"),
        P(),
        P(None, None, "gx", "gy"),
        P(None, ("gx", "gy")),
        P(("gx", "gy"), None),
        P(None, ("gx", "gy")),
        P(None, ("gx", "gy")),
        P(("gx", "gy")),
        P(("gx", "gy")),
        P(("gx", "gy")),
    )
    return jax.shard_map(
        body,
        mesh=mesh,
        in_specs=placed,
        out_specs=(P(None, "gx", "gy"), P(("gx", "gy")), P()),
        check_vma=False,
    )
```

```python
import jax
import jax.numpy as jnp
from jax import lax
from jax.experimental import pallas as pl
from jax.experimental.pallas import tpu as pltpu
from jax.sharding import PartitionSpec as P

NI = 32
STEPS = 2
LANES = 128
MAIN = 128
TAIL = 16
BLOCK = MAIN + TAIL
GROUP = 8
WIDE = 8
MIX_UNROLL = 2
FRONT = 8
POINTS = 4
PIECES = 4
VLIM = 60
EXPAND = 4
STRIDE = 37
MESH = pl.DeviceIdType.MESH
VMEM = pl.BlockSpec(memory_space=pltpu.VMEM)
SMEM = pl.BlockSpec(memory_space=pltpu.SMEM)
HBM = pl.BlockSpec(memory_space=pltpu.HBM)
MIB = 1024 * 1024


def identity(rows, dtype):
    row = lax.broadcasted_iota(jnp.int32, (rows, LANES), 0)
    col = lax.broadcasted_iota(jnp.int32, (rows, LANES), 1)
    return (row == col).astype(dtype)


def dot_nt(a, b):
    return lax.dot_general(a, b, (((1,), (1,)), ((), ())), preferred_element_type=jnp.float32)


def moved(step, sign):
    gx, gy = lax.axis_index("gx"), lax.axis_index("gy")
    z, x, y, core = gx // 4, lax.rem(gx, 4), gy // 2, lax.rem(gy, 2)
    dz, dx, dy, dc = lax.rem(step, 4), lax.rem(step // 4, 4), lax.rem(step // 16, 4), step // 64
    if sign < 0:
        dz, dx, dy = 4 - dz, 4 - dx, 4 - dy
    return (
        lax.rem(z + dz, 4) * 4 + lax.rem(x + dx, 4),
        lax.rem(y + dy, 4) * 2 + lax.rem(core + dc, 2),
    )


def peer(step):
    return moved(step, 1)


def split(value):
    high = value.astype(jnp.bfloat16)
    return high, (value - high.astype(jnp.float32)).astype(jnp.bfloat16)


def product(parts_a, parts_b):
    high_a, low_a = parts_a
    high_b, low_b = parts_b
    one = jnp.dot(high_a, high_b, preferred_element_type=jnp.float32)
    two = jnp.dot(low_a, high_b, preferred_element_type=jnp.float32)
    return one + (two + jnp.dot(high_a, low_b, preferred_element_type=jnp.float32))


def vertical_mix(levels, rows_x, coupling_t, source, mixed, beside=None):
    padded = coupling_t.shape[1]
    stacked = coupling_t[...].reshape(2 * padded, padded)
    pad = jnp.zeros((padded - levels, 2 * LANES), jnp.float32)

    @pl.loop(0, rows_x // 2, unroll=MIX_UNROLL)
    def _(t):
        x = 2 * t
        pair = jnp.concatenate(
            [source[pl.ds(x, levels, stride=rows_x), :], source[pl.ds(x + 1, levels, stride=rows_x), :]], axis=1
        )
        high, low = split(jnp.concatenate([pair, pad], axis=0))
        both = jnp.dot(stacked, high, preferred_element_type=jnp.float32)
        if beside is not None:
            beside(t)
        out = both[:padded] + (
            both[padded:] + jnp.dot(stacked[:padded], low, preferred_element_type=jnp.float32)
        )
        mixed[pl.ds(x, levels, stride=rows_x), :] = out[:levels, :LANES]
        mixed[pl.ds(x + 1, levels, stride=rows_x), :] = out[:levels, LANES:]


def by_bank(levels, work):
    for bank, first in enumerate(range(0, levels, LANES)):
        count = min(LANES, levels - first)
        whole = count // WIDE

        @pl.loop(0, whole)
        def _(t):
            work(bank, first, t * WIDE, WIDE)

        if count % WIDE:
            work(bank, first, whole * WIDE, count % WIDE)


def at_edges(lane, first, last):
    return jnp.where(lane == 0, first, jnp.where(lane == LANES - 1, last, 0.0))


def spread(levels, rows_x, transport, mixed, out, row_edge, col_edge, col_mixed, col_own):
    row = lax.broadcasted_iota(jnp.int32, (rows_x, LANES), 0)
    lane = lax.broadcasted_iota(jnp.int32, (rows_x, LANES), 1)

    def work(bank, first, spot, width):
        right_edge, left_edge = col_edge[0, bank], col_edge[1, bank]
        if col_mixed is not None:
            before_all, after_all = col_mixed[0, bank], col_mixed[1, bank]
            first_own, last_own = col_own[0, bank], col_own[1, bank]
        for i in range(width):
            at = spot + i
            l = first + at
            here = pl.ds(pl.multiple_of(l * rows_x, rows_x), rows_x)
            u = mixed[here, :]
            if col_mixed is not None:
                before = pltpu.roll(before_all, lax.rem(LANES - at, LANES), 1)
                after = pltpu.roll(after_all, LANES - 1 - at, 1)
                u = u + at_edges(lane, before, after)
            part = [transport[l, k].astype(jnp.float32) * u for k in range(5)]
            down = pltpu.roll(part[1], 1, 0)
            up = pltpu.roll(part[2], rows_x - 1, 0)
            right = pltpu.roll(part[3], 1, 1)
            left = pltpu.roll(part[4], LANES - 1, 1)
            row_edge[0, pl.ds(l, 1), :] = down[0:1]
            row_edge[1, pl.ds(l, 1), :] = up[rows_x - 1 : rows_x]
            mine = lane == at
            right_edge = jnp.where(mine, pltpu.roll(part[3], lax.rem(at + 1, LANES), 1), right_edge)
            left_edge = jnp.where(mine, pltpu.roll(part[4], at, 1), left_edge)
            total = part[0] + jnp.where(row == 0, 0.0, down) + jnp.where(row == rows_x - 1, 0.0, up)
            total = total + jnp.where(lane == 0, 0.0, right) + jnp.where(lane == LANES - 1, 0.0, left)
            out[here, :] = total
            if col_mixed is not None:
                first_own = jnp.where(mine, pltpu.roll(total, at, 1), first_own)
                last_own = jnp.where(mine, pltpu.roll(total, lax.rem(at + 1, LANES), 1), last_own)
        col_edge[0, bank] = right_edge
        col_edge[1, bank] = left_edge
        if col_mixed is not None:
            col_own[0, bank] = first_own
            col_own[1, bank] = last_own

    by_bank(levels, work)


def add_columns(levels, rows_x, out, col_halo):
    lane = lax.broadcasted_iota(jnp.int32, (rows_x, LANES), 1)

    def work(bank, start, spot, width):
        before_all, after_all = col_halo[0, bank], col_halo[1, bank]
        for i in range(width):
            at = spot + i
            here = pl.ds(pl.multiple_of((start + at) * rows_x, rows_x), rows_x)
            before = pltpu.roll(before_all, lax.rem(LANES - at, LANES), 1)
            after = pltpu.roll(after_all, LANES - 1 - at, 1)
            out[here, :] = out[here, :] + at_edges(lane, before, after)

    by_bank(levels, work)


def table_rows(levels, rows_x, field, table, x):
    eye = identity(LANES, jnp.bfloat16)
    slab = field[pl.ds(x, levels, stride=rows_x), :]
    tail = jnp.concatenate([slab[MAIN:levels], jnp.zeros((2 * MAIN - levels, LANES), jnp.float32)], axis=0)
    base = FRONT + x * 2 * LANES
    table[pl.ds(base, LANES, stride=2), :] = dot_nt(eye, slab[:MAIN].astype(jnp.bfloat16))
    table[pl.ds(base + 1, LANES, stride=2), :] = dot_nt(eye, tail.astype(jnp.bfloat16))


def whole_kernel(
    columns_in,
    valid,
    gradient_in,
    coupling_in,
    transport_in,
    jac_in,
    slots_in,
    weight_in,
    innovation_in,
    inst_in,
    field_out,
    impact,
    total,
    field,
    columns,
    gradient,
    coupling,
    transport,
    jac,
    weight,
    innovation,
    inst,
    slots_v,
    slots,
    square,
    coupling_t,
    mixed,
    row_edge,
    col_edge,
    row_halo,
    col_halo,
    col_mixed,
    col_own,
    table,
    ga,
    gb,
    outgoing,
    received,
    profiles,
    oa,
    ob,
    part,
    near_shares,
    far_shares,
    edge_send,
    edge_recv,
    send_sem,
    recv_sem,
    share_send,
    share_recv,
    local_sem,
):
    gx, gy = lax.axis_index("gx"), lax.axis_index("gy")
    nx, ny = lax.axis_size("gx"), lax.axis_size("gy")
    me = gx * ny + gy
    ranks = received.shape[0]
    levels = coupling.shape[0]
    rows_x = field.shape[0] // levels
    padded = coupling_t.shape[1]
    chunks = impact.shape[0]
    barrier = pltpu.get_barrier_semaphore()

    loads = [
        pltpu.make_async_copy(source, target, local_sem.at[4 + i])
        for i, (source, target) in enumerate(
            (
                (coupling_in, coupling),
                (gradient_in, gradient),
                (transport_in, transport),
                (slots_in, slots_v),
                (columns_in, columns),
                (jac_in, jac),
                (weight_in, weight),
                (innovation_in, innovation),
                (inst_in, inst),
            )
        )
    ]
    for load in loads:
        load.start()
    load_coupling, load_gradient, load_transport, load_lines, load_columns = loads[:5]

    def greet(k):
        pl.semaphore_signal(barrier, inc=1, device_id=peer(k), device_id_type=MESH)

    share_of = ranks // (rows_x // 2)
    for k in range(share_of, ranks, share_of):
        greet(k)

    def greet_some(t):
        for i in range(1, share_of):
            greet(t * share_of + i)

    square[...] = jnp.zeros_like(square)
    load_coupling.wait()
    square[0:levels, 0:levels] = coupling[...]
    coupling_parts = split(square[...])
    side = square.shape[0]
    wide_eye = (
        lax.broadcasted_iota(jnp.int32, (padded, side), 0) == lax.broadcasted_iota(jnp.int32, (padded, side), 1)
    ).astype(jnp.bfloat16)
    for i in range(2):
        coupling_t[i] = dot_nt(wide_eye, coupling_parts[i])[:, :padded].astype(jnp.bfloat16)
    col_edge[...] = jnp.zeros_like(col_edge)
    col_own[...] = jnp.zeros_like(col_own)
    table[0:FRONT, :] = jnp.zeros((FRONT, LANES), jnp.float32)

    sides = (
        (row_edge, row_halo, 0, (lax.rem(gx + 1, nx), gy)),
        (row_edge, row_halo, 1, (lax.rem(gx + nx - 1, nx), gy)),
        (col_edge, col_halo, 0, (gx, lax.rem(gy + 1, ny))),
        (col_edge, col_halo, 1, (gx, lax.rem(gy + ny - 1, ny))),
    )
    inside = (gx > 0, gx < nx - 1, gy > 0, gy < ny - 1)
    ends = (pl.ds(0, levels, stride=rows_x), pl.ds(rows_x - 1, levels, stride=rows_x))

    def edge_copies(step):
        return [
            pltpu.make_async_remote_copy(
                src_ref=edge.at[step, which],
                dst_ref=halo.at[step, which],
                send_sem=edge_send.at[step, i],
                recv_sem=edge_recv.at[step, i],
                device_id=device,
                device_id_type=MESH,
            )
            for i, (edge, halo, which, device) in enumerate(sides)
        ]

    def row_values(step, which):
        return jnp.where(inside[which], row_halo[step, which, 0:levels, :], 0.0)

    load_gradient.wait()
    vertical_mix(levels, rows_x, coupling_t, gradient, mixed, greet_some)
    load_transport.wait()
    spread(levels, rows_x, transport, mixed, field, row_edge.at[0], col_edge.at[0], None, None)
    pl.semaphore_wait(barrier, ranks - 1)
    copies = edge_copies(0)
    for copy in copies:
        copy.start()
    vertical_mix(levels, rows_x, coupling_t, field, mixed)
    for copy in copies:
        copy.wait()
    both = jnp.concatenate([row_values(0, 0), row_values(0, 1)], axis=1)
    both = jnp.concatenate([both, jnp.zeros((padded - levels, 2 * LANES), jnp.float32)], axis=0)
    added = product((coupling_t[0], coupling_t[1]), split(both))
    for which in range(2):
        mixed[ends[which], :] = mixed[ends[which], :] + added[:levels, which * LANES : (which + 1) * LANES]
    strips = jnp.concatenate(
        [
            jnp.where(inside[2 + which], jnp.concatenate([col_halo[0, which, 0], col_halo[0, which, 1]], axis=1), 0.0)
            for which in range(2)
        ],
        axis=0,
    )
    strips = product(split(strips), coupling_parts)
    for which in range(2):
        for bank in range(2):
            col_mixed[which, bank] = strips[
                which * rows_x : (which + 1) * rows_x, bank * LANES : (bank + 1) * LANES
            ]

    spread(levels, rows_x, transport, mixed, field, row_edge.at[1], col_edge.at[1], col_mixed, col_own)
    copies = edge_copies(1)
    for copy in copies:
        copy.start()

    @pl.loop(0, (rows_x - 2) // 3)
    def _(t):
        for i in range(3):
            table_rows(levels, rows_x, field, table, 1 + t * 3 + i)

    load_lines.wait()
    slots_v[...] = slots_v[...] * 2
    load_columns.wait()
    load_slots = pltpu.make_async_copy(slots_v, slots, local_sem.at[2])
    load_slots.start()
    for copy in copies:
        copy.wait()
    corners = (
        (lax.broadcasted_iota(jnp.int32, (8, LANES), 0) * (LANES - 1) == lax.broadcasted_iota(jnp.int32, (8, LANES), 1))
        & (lax.broadcasted_iota(jnp.int32, (8, LANES), 0) < 2)
    ).astype(jnp.float32)
    for which in range(2):
        x = which * (rows_x - 1)
        halo = row_values(1, which)
        field[ends[which], :] = field[ends[which], :] + halo
        table_rows(levels, rows_x, field, table, x)
        halo = jnp.concatenate([halo, jnp.zeros((side - levels, LANES), jnp.float32)], axis=0)
        crossing = lax.dot_general(
            corners,
            halo,
            (((1,), (1,)), ((), ())),
            precision=lax.Precision.HIGHEST,
            preferred_element_type=jnp.float32,
        )
        for end in range(2):
            for bank in range(2):
                spot = col_own.at[end, bank]
                spot[x : x + 1, :] = spot[x : x + 1, :] + crossing[end : end + 1, bank * LANES : (bank + 1) * LANES]
    for end in range(2):
        for bank in range(2):
            strip = jnp.where(inside[2 + end], col_halo[1, end, bank], 0.0)
            col_mixed[end, bank] = strip
            table[pl.ds(FRONT + end * 2 * (LANES - 1) + bank, rows_x, stride=2 * LANES), :] = col_own[end, bank] + strip

    pick = identity(TAIL, jnp.bfloat16)

    def step_at(k):
        return lax.rem((k + 1) * STRIDE, ranks)

    def owner_at(k):
        tx, ty = peer(step_at(k))
        return tx * ny + ty

    def copy_for(k):
        step = step_at(k)
        tx, ty = peer(step)
        return pltpu.make_async_remote_copy(
            src_ref=outgoing.at[tx * ny + ty],
            dst_ref=received.at[me],
            send_sem=send_sem,
            recv_sem=recv_sem.at[step],
            device_id=(tx, ty),
            device_id_type=MESH,
        )

    def gather(k, rows):
        base = owner_at(k) * LANES
        for i in range(0, LANES, GROUP):
            got = [table[pl.ds(columns[base + i + j] * 2 + FRONT, 2), :] for j in range(GROUP)]
            for j in range(GROUP):
                rows[pl.ds((i + j) * 2, 2), :] = got[j]

    def pack(k, rows, next_k, next_rows):
        owner = owner_at(k)
        main = rows[pl.ds(0, LANES, stride=2), :].astype(jnp.bfloat16)
        tail = rows[pl.ds(1, LANES, stride=2), :].astype(jnp.bfloat16)
        packed = dot_nt(pick, tail)
        gather(next_k, next_rows)
        outgoing[owner, 0:MAIN, :] = main
        outgoing[owner, MAIN:BLOCK, :] = packed.astype(jnp.bfloat16)

    gather(0, ga)

    @pl.loop(0, ranks // 2)
    def _(t):
        k = t * 2
        pack(k, ga, k + 1, gb)
        copy_for(k).start()
        pack(k + 1, gb, jnp.minimum(k + 2, ranks - 1), ga)

        @pl.when(k + 1 < ranks - 1)
        def _():
            copy_for(k + 1).start()

    own = pltpu.make_async_copy(outgoing.at[me], received.at[me], local_sem.at[3])
    own.start()

    add_columns(levels, rows_x, field, col_mixed)
    store_field = pltpu.make_async_copy(field, field_out, local_sem.at[0])
    store_field.start()
    part[...] = jnp.zeros_like(part)
    for load in loads[5:]:
        load.wait()
    load_slots.wait()
    own.wait()

    spread_tail = identity(TAIL, jnp.bfloat16)

    def expand(h):
        base = pl.multiple_of(h * 2 * LANES, 2 * LANES)
        profiles[pl.ds(base, LANES, stride=2), :] = received[h, 0:MAIN, :].astype(jnp.float32)
        profiles[pl.ds(base + 1, LANES, stride=2), :] = lax.dot_general(
            received[h, MAIN:BLOCK, :], spread_tail, (((0,), (0,)), ((), ())), preferred_element_type=jnp.float32
        )

    def holder_at(k):
        hx, hy = moved(step_at(k), -1)
        return hx * ny + hy

    @pl.loop(0, ranks // EXPAND)
    def _(t):
        for i in range(EXPAND):
            k = t * EXPAND + i

            @pl.when(k < ranks - 1)
            def _():
                copy_for(k).wait_recv()

        for i in range(EXPAND):
            expand(holder_at(t * EXPAND + i))

    eye = identity(LANES, jnp.int32) == 1
    lane = lax.broadcasted_iota(jnp.int32, (1, LANES), 1)

    def fetch(j, rows, c, first, count):
        line = j * POINTS + c
        for i in range(first, first + count, GROUP):
            got = [profiles[pl.ds(slots[line, i + k], 2), :] for k in range(GROUP)]
            for k in range(GROUP):
                rows[pl.ds((c * LANES + i + k) * 2, 2), :] = got[k]

    def work(j, rows, next_j, next_rows):
        col = pl.multiple_of(j * LANES, LANES)
        tail = jnp.concatenate(
            [
                jac[MAIN:levels, pl.ds(col, LANES)].astype(jnp.float32),
                jnp.zeros((BLOCK - levels, LANES), jnp.float32),
            ],
            axis=0,
        ).astype(jnp.bfloat16)
        profile = jnp.concatenate(
            [jac[0:MAIN, pl.ds(col, LANES)], tail, jnp.zeros((2 * MAIN - BLOCK, LANES), jnp.bfloat16)], axis=0
        )
        value = jnp.zeros((1, LANES), jnp.float32)
        for c in range(POINTS):
            main = rows[pl.ds(c * 2 * LANES, LANES, stride=2), :].astype(jnp.bfloat16)
            rest = rows[pl.ds(c * 2 * LANES + 1, LANES, stride=2), :].astype(jnp.bfloat16)
            products = jnp.dot(
                jnp.concatenate([main, rest], axis=1), profile, preferred_element_type=jnp.float32
            )
            fetch(next_j, next_rows, c, 0, LANES // 2)
            diagonal = jnp.sum(jnp.where(eye, products, 0.0), axis=0, keepdims=True)
            value = value + diagonal * weight[c : c + 1, pl.ds(col, LANES)]
            fetch(next_j, next_rows, c, LANES // 2, LANES // 2)
        value = innovation[pl.ds(j, 1), :] * value
        value = jnp.where(lane + j * LANES < valid[0], value, 0.0)
        impact[pl.ds(j, 1), :] = value
        same = lax.broadcasted_iota(jnp.int32, (NI, LANES), 0) == inst[pl.ds(j, 1), :]
        part[...] += jnp.where(same, value, 0.0)

    for c in range(POINTS):
        fetch(0, oa, c, 0, LANES)

    @pl.loop(0, chunks // 2)
    def _(t):
        j = t * 2
        work(j, oa, j + 1, ob)
        work(j + 1, ob, jnp.minimum(j + 2, chunks - 1), oa)

    pltpu.make_async_remote_copy(
        src_ref=outgoing.at[pl.ds(0, ranks - 1)],
        dst_ref=received.at[pl.ds(0, ranks - 1)],
        send_sem=send_sem,
        recv_sem=recv_sem.at[0],
        device_id=peer(1),
        device_id_type=MESH,
    ).wait_send()

    rows = lax.dot_general(
        jnp.ones((8, LANES), jnp.float32),
        part[...],
        (((1,), (1,)), ((), ())),
        precision=lax.Precision.HIGHEST,
        preferred_element_type=jnp.float32,
    )
    own_rows = jnp.concatenate([rows, jnp.zeros((8, LANES - NI), jnp.float32)], axis=1)

    def share(value, slots_at, size, mine, device, base):
        slots_at[mine] = value
        shared = [
            pltpu.make_async_remote_copy(
                src_ref=slots_at.at[mine],
                dst_ref=slots_at.at[mine],
                send_sem=share_send.at[base + k],
                recv_sem=share_recv.at[base + k],
                device_id=device(lax.rem(mine + k, size)),
                device_id_type=MESH,
            )
            for k in range(1, size)
        ]
        for copy in shared:
            copy.start()
        for copy in shared:
            copy.wait()
        return jnp.sum(slots_at[...], axis=0)

    store_field.wait()
    near = share(own_rows, near_shares, ny, gy, lambda i: (gx, i), 0)
    total[...] = share(near, far_shares, nx, gx, lambda i: (i, gy), ny)[0:1, :NI]


def run(columns, valid, gradient, coupling, transport, jac, slots, weight, innovation, inst, nx, ny):
    ranks = nx * ny
    levels, rows_x, lanes = gradient.shape
    count = innovation.shape[0]
    chunks = count // LANES
    flat = gradient.reshape(levels * rows_x, lanes)
    padded = -(-levels // TAIL) * TAIL
    slots = slots.reshape(POINTS, chunks, LANES).transpose(1, 0, 2).reshape(chunks * POINTS, LANES)
    f32, bf16 = jnp.float32, jnp.bfloat16
    row_edges = pltpu.VMEM((STEPS, 2, padded, LANES), f32)
    col_edges = pltpu.VMEM((STEPS, 2, 2, rows_x, LANES), f32)
    block = pltpu.VMEM((ranks, BLOCK, LANES), bf16)
    field, impact, total = pl.pallas_call(
        whole_kernel,
        out_shape=(
            jax.ShapeDtypeStruct(flat.shape, f32),
            jax.ShapeDtypeStruct((chunks, LANES), f32),
            jax.ShapeDtypeStruct((1, NI), f32),
        ),
        in_specs=[HBM, SMEM] + [HBM] * 8,
        out_specs=(HBM, VMEM, VMEM),
        scratch_shapes=[
            pltpu.VMEM(flat.shape, f32),
            pltpu.SMEM(columns.shape, jnp.int32),
            pltpu.VMEM(flat.shape, f32),
            pltpu.VMEM(coupling.shape, f32),
            pltpu.VMEM(transport.shape, bf16),
            pltpu.VMEM(jac.shape, bf16),
            pltpu.VMEM(weight.shape, f32),
            pltpu.VMEM((chunks, LANES), f32),
            pltpu.VMEM((chunks, LANES), jnp.int32),
            pltpu.VMEM(slots.shape, jnp.int32),
            pltpu.SMEM(slots.shape, jnp.int32),
            pltpu.VMEM((2 * MAIN, 2 * MAIN), f32),
            pltpu.VMEM((2, padded, padded), bf16),
            pltpu.VMEM(flat.shape, f32),
            row_edges,
            col_edges,
            row_edges,
            col_edges,
            pltpu.VMEM((2, 2, rows_x, LANES), f32),
            pltpu.VMEM((2, 2, rows_x, LANES), f32),
            pltpu.VMEM((FRONT + rows_x * lanes * 2, LANES), f32),
            pltpu.VMEM((2 * LANES, LANES), f32),
            pltpu.VMEM((2 * LANES, LANES), f32),
            block,
            block,
            pltpu.VMEM((ranks * 2 * LANES, LANES), f32),
            pltpu.VMEM((POINTS * 2 * LANES, LANES), f32),
            pltpu.VMEM((POINTS * 2 * LANES, LANES), f32),
            pltpu.VMEM((NI, LANES), f32),
            pltpu.VMEM((ny, 8, LANES), f32),
            pltpu.VMEM((nx, 8, LANES), f32),
            pltpu.SemaphoreType.DMA((STEPS, 4)),
            pltpu.SemaphoreType.DMA((STEPS, 4)),
            pltpu.SemaphoreType.DMA,
            pltpu.SemaphoreType.DMA((ranks,)),
            pltpu.SemaphoreType.DMA((nx + ny,)),
            pltpu.SemaphoreType.DMA((nx + ny,)),
            pltpu.SemaphoreType.DMA((13,)),
        ],
        compiler_params=pltpu.CompilerParams(collective_id=1, has_side_effects=True, vmem_limit_bytes=VLIM * MIB),
        name="whole",
    )(
        columns,
        valid,
        flat,
        coupling,
        transport,
        jac,
        slots,
        weight,
        innovation.reshape(chunks, LANES),
        inst.reshape(chunks, LANES),
    )
    field, impact, total = finish(field, impact, total)
    return field.reshape(gradient.shape), impact.reshape(count), total.reshape(NI)


def finish_kernel(field, impact, total, field_out, impact_out, total_out, held, in_sem, out_sem):
    size = field.shape[0] // PIECES
    cuts = [pl.ds(i * size, size) for i in range(PIECES)]
    ins = [pltpu.make_async_copy(field.at[cut], held.at[cut], in_sem.at[i]) for i, cut in enumerate(cuts)]
    outs = [pltpu.make_async_copy(held.at[cut], field_out.at[cut], out_sem.at[i]) for i, cut in enumerate(cuts)]
    for copy in ins:
        copy.start()
    impact_out[...] = impact[...]
    total_out[...] = total[...]
    for come, go in zip(ins, outs):
        come.wait()
        go.start()
    for copy in outs:
        copy.wait()


def finish(field, impact, total):
    return pl.pallas_call(
        finish_kernel,
        out_shape=tuple(jax.ShapeDtypeStruct(a.shape, a.dtype) for a in (field, impact, total)),
        in_specs=[HBM, VMEM, VMEM],
        out_specs=(HBM, VMEM, VMEM),
        scratch_shapes=[
            pltpu.VMEM(field.shape, field.dtype),
            pltpu.SemaphoreType.DMA((PIECES,)),
            pltpu.SemaphoreType.DMA((PIECES,)),
        ],
        compiler_params=pltpu.CompilerParams(vmem_limit_bytes=VLIM * MIB),
        name="finish",
    )(field, impact, total)


def body(
    gradient,
    coupling,
    transport,
    obs_jacobian,
    send_cols,
    obs_slots,
    obs_weight,
    obs_inst,
    innovation,
    valid_count,
):
    return run(
        send_cols[0],
        valid_count,
        gradient,
        coupling,
        transport,
        obs_jacobian,
        obs_slots,
        obs_weight,
        innovation,
        obs_inst,
        lax.axis_size("gx"),
        lax.axis_size("gy"),
    )


def solution(mesh):
    placed = (
        P(None, "gx", "gy"),
        P(),
        P(None, None, "gx", "gy"),
        P(None, ("gx", "gy")),
        P(("gx", "gy"), None),
        P(None, ("gx", "gy")),
        P(None, ("gx", "gy")),
        P(("gx", "gy")),
        P(("gx", "gy")),
        P(("gx", "gy")),
    )
    return jax.shard_map(
        body,
        mesh=mesh,
        in_specs=placed,
        out_specs=(P(None, "gx", "gy"), P(("gx", "gy")), P()),
        check_vma=False,
    )
```

```python
import jax
import jax.numpy as jnp
from jax import lax
from jax.experimental import pallas as pl
from jax.experimental.pallas import tpu as pltpu
from jax.sharding import PartitionSpec as P

NI = 32
STEPS = 2
LANES = 128
MAIN = 128
TAIL = 16
BLOCK = MAIN + TAIL
GROUP = 8
WIDE = 8
MIX_UNROLL = 4
FRONT = 8
POINTS = 4
PIECES = 4
VLIM = 60
EXPAND = 4
STRIDE = 37
MESH = pl.DeviceIdType.MESH
VMEM = pl.BlockSpec(memory_space=pltpu.VMEM)
SMEM = pl.BlockSpec(memory_space=pltpu.SMEM)
HBM = pl.BlockSpec(memory_space=pltpu.HBM)
MIB = 1024 * 1024


def identity(rows, dtype):
    row = lax.broadcasted_iota(jnp.int32, (rows, LANES), 0)
    col = lax.broadcasted_iota(jnp.int32, (rows, LANES), 1)
    return (row == col).astype(dtype)


def dot_nt(a, b):
    return lax.dot_general(a, b, (((1,), (1,)), ((), ())), preferred_element_type=jnp.float32)


def moved(step, sign):
    gx, gy = lax.axis_index("gx"), lax.axis_index("gy")
    z, x, y, core = gx // 4, lax.rem(gx, 4), gy // 2, lax.rem(gy, 2)
    dz, dx, dy, dc = lax.rem(step, 4), lax.rem(step // 4, 4), lax.rem(step // 16, 4), step // 64
    if sign < 0:
        dz, dx, dy = 4 - dz, 4 - dx, 4 - dy
    return (
        lax.rem(z + dz, 4) * 4 + lax.rem(x + dx, 4),
        lax.rem(y + dy, 4) * 2 + lax.rem(core + dc, 2),
    )


def peer(step):
    return moved(step, 1)


def split(value):
    high = value.astype(jnp.bfloat16)
    return high, (value - high.astype(jnp.float32)).astype(jnp.bfloat16)


def product(parts_a, parts_b):
    high_a, low_a = parts_a
    high_b, low_b = parts_b
    one = jnp.dot(high_a, high_b, preferred_element_type=jnp.float32)
    two = jnp.dot(low_a, high_b, preferred_element_type=jnp.float32)
    return one + (two + jnp.dot(high_a, low_b, preferred_element_type=jnp.float32))


def vertical_mix(levels, rows_x, coupling_t, source, mixed, beside=None):
    padded = coupling_t.shape[1]
    stacked = coupling_t[...].reshape(2 * padded, padded)
    pad = jnp.zeros((padded - levels, 2 * LANES), jnp.float32)

    @pl.loop(0, rows_x // 2, unroll=MIX_UNROLL)
    def _(t):
        x = 2 * t
        pair = jnp.concatenate(
            [source[pl.ds(x, levels, stride=rows_x), :], source[pl.ds(x + 1, levels, stride=rows_x), :]], axis=1
        )
        high, low = split(jnp.concatenate([pair, pad], axis=0))
        both = jnp.dot(stacked, high, preferred_element_type=jnp.float32)
        if beside is not None:
            beside(t)
        out = both[:padded] + (
            both[padded:] + jnp.dot(stacked[:padded], low, preferred_element_type=jnp.float32)
        )
        mixed[pl.ds(x, levels, stride=rows_x), :] = out[:levels, :LANES]
        mixed[pl.ds(x + 1, levels, stride=rows_x), :] = out[:levels, LANES:]


def by_bank(levels, work, wide):
    for bank, first in enumerate(range(0, levels, LANES)):
        count = min(LANES, levels - first)
        whole = count // wide

        @pl.loop(0, whole)
        def _(t):
            work(bank, first, t * wide, wide)

        if count % wide:
            work(bank, first, whole * wide, count % wide)


def at_edges(lane, first, last):
    return jnp.where(lane == 0, first, jnp.where(lane == LANES - 1, last, 0.0))


def spread(levels, rows_x, transport, mixed, out, row_edge, col_edge, col_mixed, col_own):
    row = lax.broadcasted_iota(jnp.int32, (rows_x, LANES), 0)
    lane = lax.broadcasted_iota(jnp.int32, (rows_x, LANES), 1)

    def work(bank, first, spot, width):
        right_edge, left_edge = col_edge[0, bank], col_edge[1, bank]
        if col_mixed is not None:
            before_all, after_all = col_mixed[0, bank], col_mixed[1, bank]
            first_own, last_own = col_own[0, bank], col_own[1, bank]
        for i in range(width):
            at = spot + i
            l = first + at
            here = pl.ds(pl.multiple_of(l * rows_x, rows_x), rows_x)
            u = mixed[here, :]
            if col_mixed is not None:
                before = pltpu.roll(before_all, lax.rem(LANES - at, LANES), 1)
                after = pltpu.roll(after_all, LANES - 1 - at, 1)
                u = u + at_edges(lane, before, after)
            part = [transport[l, k].astype(jnp.float32) * u for k in range(5)]
            down = pltpu.roll(part[1], 1, 0)
            up = pltpu.roll(part[2], rows_x - 1, 0)
            right = pltpu.roll(part[3], 1, 1)
            left = pltpu.roll(part[4], LANES - 1, 1)
            row_edge[0, pl.ds(l, 1), :] = down[0:1]
            row_edge[1, pl.ds(l, 1), :] = up[rows_x - 1 : rows_x]
            mine = lane == at
            right_edge = jnp.where(mine, pltpu.roll(part[3], lax.rem(at + 1, LANES), 1), right_edge)
            left_edge = jnp.where(mine, pltpu.roll(part[4], at, 1), left_edge)
            total = part[0] + jnp.where(row == 0, 0.0, down) + jnp.where(row == rows_x - 1, 0.0, up)
            total = total + jnp.where(lane == 0, 0.0, right) + jnp.where(lane == LANES - 1, 0.0, left)
            out[here, :] = total
            if col_mixed is not None:
                first_own = jnp.where(mine, pltpu.roll(total, at, 1), first_own)
                last_own = jnp.where(mine, pltpu.roll(total, lax.rem(at + 1, LANES), 1), last_own)
        col_edge[0, bank] = right_edge
        col_edge[1, bank] = left_edge
        if col_mixed is not None:
            col_own[0, bank] = first_own
            col_own[1, bank] = last_own

    by_bank(levels, work, WIDE if col_mixed is None else WIDE // 2)


def add_columns(levels, rows_x, out, col_halo):
    lane = lax.broadcasted_iota(jnp.int32, (rows_x, LANES), 1)

    def work(bank, start, spot, width):
        before_all, after_all = col_halo[0, bank], col_halo[1, bank]
        for i in range(width):
            at = spot + i
            here = pl.ds(pl.multiple_of((start + at) * rows_x, rows_x), rows_x)
            before = pltpu.roll(before_all, lax.rem(LANES - at, LANES), 1)
            after = pltpu.roll(after_all, LANES - 1 - at, 1)
            out[here, :] = out[here, :] + at_edges(lane, before, after)

    by_bank(levels, work, WIDE)


def table_rows(levels, rows_x, field, table, x):
    eye = identity(LANES, jnp.bfloat16)
    slab = field[pl.ds(x, levels, stride=rows_x), :]
    tail = jnp.concatenate([slab[MAIN:levels], jnp.zeros((2 * MAIN - levels, LANES), jnp.float32)], axis=0)
    base = FRONT + x * 2 * LANES
    table[pl.ds(base, LANES, stride=2), :] = dot_nt(eye, slab[:MAIN].astype(jnp.bfloat16))
    table[pl.ds(base + 1, LANES, stride=2), :] = dot_nt(eye, tail.astype(jnp.bfloat16))


def whole_kernel(
    columns_in,
    valid,
    gradient_in,
    coupling_in,
    transport_in,
    jac_in,
    slots_in,
    weight_in,
    innovation_in,
    inst_in,
    field_out,
    impact,
    total,
    field,
    columns,
    gradient,
    coupling,
    transport,
    jac,
    weight,
    innovation,
    inst,
    slots_v,
    slots,
    square,
    coupling_t,
    mixed,
    row_edge,
    col_edge,
    row_halo,
    col_halo,
    col_mixed,
    col_own,
    table,
    ga,
    gb,
    outgoing,
    received,
    profiles,
    oa,
    ob,
    part,
    near_shares,
    far_shares,
    edge_send,
    edge_recv,
    send_sem,
    recv_sem,
    share_send,
    share_recv,
    local_sem,
):
    gx, gy = lax.axis_index("gx"), lax.axis_index("gy")
    nx, ny = lax.axis_size("gx"), lax.axis_size("gy")
    me = gx * ny + gy
    ranks = received.shape[0]
    levels = coupling.shape[0]
    rows_x = field.shape[0] // levels
    padded = coupling_t.shape[1]
    chunks = impact.shape[0]
    barrier = pltpu.get_barrier_semaphore()

    loads = [
        pltpu.make_async_copy(source, target, local_sem.at[4 + i])
        for i, (source, target) in enumerate(
            (
                (coupling_in, coupling),
                (gradient_in, gradient),
                (transport_in, transport),
                (slots_in, slots_v),
                (columns_in, columns),
                (jac_in, jac),
                (weight_in, weight),
                (innovation_in, innovation),
                (inst_in, inst),
            )
        )
    ]
    for load in loads:
        load.start()
    load_coupling, load_gradient, load_transport, load_lines, load_columns = loads[:5]

    def greet(k):
        pl.semaphore_signal(barrier, inc=1, device_id=peer(k), device_id_type=MESH)

    share_of = ranks // (rows_x // 2)
    for k in range(share_of, ranks, share_of):
        greet(k)

    def greet_some(t):
        for i in range(1, share_of):
            greet(t * share_of + i)

    square[...] = jnp.zeros_like(square)
    load_coupling.wait()
    square[0:levels, 0:levels] = coupling[...]
    coupling_parts = split(square[...])
    side = square.shape[0]
    wide_eye = (
        lax.broadcasted_iota(jnp.int32, (padded, side), 0) == lax.broadcasted_iota(jnp.int32, (padded, side), 1)
    ).astype(jnp.bfloat16)
    for i in range(2):
        coupling_t[i] = dot_nt(wide_eye, coupling_parts[i])[:, :padded].astype(jnp.bfloat16)
    col_edge[...] = jnp.zeros_like(col_edge)
    col_own[...] = jnp.zeros_like(col_own)
    table[0:FRONT, :] = jnp.zeros((FRONT, LANES), jnp.float32)

    sides = (
        (row_edge, row_halo, 0, (lax.rem(gx + 1, nx), gy)),
        (row_edge, row_halo, 1, (lax.rem(gx + nx - 1, nx), gy)),
        (col_edge, col_halo, 0, (gx, lax.rem(gy + 1, ny))),
        (col_edge, col_halo, 1, (gx, lax.rem(gy + ny - 1, ny))),
    )
    inside = (gx > 0, gx < nx - 1, gy > 0, gy < ny - 1)
    ends = (pl.ds(0, levels, stride=rows_x), pl.ds(rows_x - 1, levels, stride=rows_x))

    def edge_copies(step):
        return [
            pltpu.make_async_remote_copy(
                src_ref=edge.at[step, which],
                dst_ref=halo.at[step, which],
                send_sem=edge_send.at[step, i],
                recv_sem=edge_recv.at[step, i],
                device_id=device,
                device_id_type=MESH,
            )
            for i, (edge, halo, which, device) in enumerate(sides)
        ]

    def row_values(step, which):
        return jnp.where(inside[which], row_halo[step, which, 0:levels, :], 0.0)

    load_gradient.wait()
    vertical_mix(levels, rows_x, coupling_t, gradient, mixed, greet_some)
    load_transport.wait()
    spread(levels, rows_x, transport, mixed, field, row_edge.at[0], col_edge.at[0], None, None)
    pl.semaphore_wait(barrier, ranks - 1)
    copies = edge_copies(0)
    for copy in copies:
        copy.start()
    vertical_mix(levels, rows_x, coupling_t, field, mixed)
    for copy in copies:
        copy.wait()
    both = jnp.concatenate([row_values(0, 0), row_values(0, 1)], axis=1)
    both = jnp.concatenate([both, jnp.zeros((padded - levels, 2 * LANES), jnp.float32)], axis=0)
    added = product((coupling_t[0], coupling_t[1]), split(both))
    for which in range(2):
        mixed[ends[which], :] = mixed[ends[which], :] + added[:levels, which * LANES : (which + 1) * LANES]
    strips = jnp.concatenate(
        [
            jnp.where(inside[2 + which], jnp.concatenate([col_halo[0, which, 0], col_halo[0, which, 1]], axis=1), 0.0)
            for which in range(2)
        ],
        axis=0,
    )
    strips = product(split(strips), coupling_parts)
    for which in range(2):
        for bank in range(2):
            col_mixed[which, bank] = strips[
                which * rows_x : (which + 1) * rows_x, bank * LANES : (bank + 1) * LANES
            ]

    spread(levels, rows_x, transport, mixed, field, row_edge.at[1], col_edge.at[1], col_mixed, col_own)
    copies = edge_copies(1)
    for copy in copies:
        copy.start()

    @pl.loop(0, (rows_x - 2) // 3)
    def _(t):
        for i in range(3):
            table_rows(levels, rows_x, field, table, 1 + t * 3 + i)

    load_lines.wait()
    slots_v[...] = slots_v[...] * 2
    load_columns.wait()
    load_slots = pltpu.make_async_copy(slots_v, slots, local_sem.at[2])
    load_slots.start()
    for copy in copies:
        copy.wait()
    corners = (
        (lax.broadcasted_iota(jnp.int32, (8, LANES), 0) * (LANES - 1) == lax.broadcasted_iota(jnp.int32, (8, LANES), 1))
        & (lax.broadcasted_iota(jnp.int32, (8, LANES), 0) < 2)
    ).astype(jnp.float32)
    for which in range(2):
        x = which * (rows_x - 1)
        halo = row_values(1, which)
        field[ends[which], :] = field[ends[which], :] + halo
        table_rows(levels, rows_x, field, table, x)
        halo = jnp.concatenate([halo, jnp.zeros((side - levels, LANES), jnp.float32)], axis=0)
        crossing = lax.dot_general(
            corners,
            halo,
            (((1,), (1,)), ((), ())),
            precision=lax.Precision.HIGHEST,
            preferred_element_type=jnp.float32,
        )
        for end in range(2):
            for bank in range(2):
                spot = col_own.at[end, bank]
                spot[x : x + 1, :] = spot[x : x + 1, :] + crossing[end : end + 1, bank * LANES : (bank + 1) * LANES]
    for end in range(2):
        for bank in range(2):
            strip = jnp.where(inside[2 + end], col_halo[1, end, bank], 0.0)
            col_mixed[end, bank] = strip
            table[pl.ds(FRONT + end * 2 * (LANES - 1) + bank, rows_x, stride=2 * LANES), :] = col_own[end, bank] + strip

    pick = identity(TAIL, jnp.bfloat16)

    def step_at(k):
        return lax.rem((k + 1) * STRIDE, ranks)

    def owner_at(k):
        tx, ty = peer(step_at(k))
        return tx * ny + ty

    def copy_for(k):
        step = step_at(k)
        tx, ty = peer(step)
        return pltpu.make_async_remote_copy(
            src_ref=outgoing.at[tx * ny + ty],
            dst_ref=received.at[me],
            send_sem=send_sem,
            recv_sem=recv_sem.at[step],
            device_id=(tx, ty),
            device_id_type=MESH,
        )

    def gather(k, rows):
        base = owner_at(k) * LANES
        for i in range(0, LANES, GROUP):
            got = [table[pl.ds(columns[base + i + j] * 2 + FRONT, 2), :] for j in range(GROUP)]
            for j in range(GROUP):
                rows[pl.ds((i + j) * 2, 2), :] = got[j]

    def pack(k, rows, next_k, next_rows):
        owner = owner_at(k)
        main = rows[pl.ds(0, LANES, stride=2), :].astype(jnp.bfloat16)
        tail = rows[pl.ds(1, LANES, stride=2), :].astype(jnp.bfloat16)
        packed = dot_nt(pick, tail)
        gather(next_k, next_rows)
        outgoing[owner, 0:MAIN, :] = main
        outgoing[owner, MAIN:BLOCK, :] = packed.astype(jnp.bfloat16)

    gather(0, ga)

    @pl.loop(0, ranks // 2)
    def _(t):
        k = t * 2
        pack(k, ga, k + 1, gb)
        copy_for(k).start()
        pack(k + 1, gb, jnp.minimum(k + 2, ranks - 1), ga)

        @pl.when(k + 1 < ranks - 1)
        def _():
            copy_for(k + 1).start()

    own = pltpu.make_async_copy(outgoing.at[me], received.at[me], local_sem.at[3])
    own.start()

    add_columns(levels, rows_x, field, col_mixed)
    store_field = pltpu.make_async_copy(field, field_out, local_sem.at[0])
    store_field.start()
    part[...] = jnp.zeros_like(part)
    for load in loads[5:]:
        load.wait()
    load_slots.wait()
    own.wait()

    spread_tail = identity(TAIL, jnp.bfloat16)

    def expand(h):
        base = pl.multiple_of(h * 2 * LANES, 2 * LANES)
        profiles[pl.ds(base, LANES, stride=2), :] = received[h, 0:MAIN, :].astype(jnp.float32)
        profiles[pl.ds(base + 1, LANES, stride=2), :] = lax.dot_general(
            received[h, MAIN:BLOCK, :], spread_tail, (((0,), (0,)), ((), ())), preferred_element_type=jnp.float32
        )

    def holder_at(k):
        hx, hy = moved(step_at(k), -1)
        return hx * ny + hy

    @pl.loop(0, ranks // EXPAND)
    def _(t):
        for i in range(EXPAND):
            k = t * EXPAND + i

            @pl.when(k < ranks - 1)
            def _():
                copy_for(k).wait_recv()

        for i in range(EXPAND):
            expand(holder_at(t * EXPAND + i))

    eye = identity(LANES, jnp.int32) == 1
    lane = lax.broadcasted_iota(jnp.int32, (1, LANES), 1)

    def fetch(j, rows, c, first, count):
        line = j * (POINTS * LANES) + c * LANES
        for i in range(first, first + count, GROUP):
            got = [profiles[pl.ds(slots[line + i + k], 2), :] for k in range(GROUP)]
            for k in range(GROUP):
                rows[pl.ds((c * LANES + i + k) * 2, 2), :] = got[k]

    def work(j, rows, next_j, next_rows):
        col = pl.multiple_of(j * LANES, LANES)
        tail = jnp.concatenate(
            [
                jac[MAIN:levels, pl.ds(col, LANES)].astype(jnp.float32),
                jnp.zeros((BLOCK - levels, LANES), jnp.float32),
            ],
            axis=0,
        ).astype(jnp.bfloat16)
        profile = jnp.concatenate(
            [jac[0:MAIN, pl.ds(col, LANES)], tail, jnp.zeros((2 * MAIN - BLOCK, LANES), jnp.bfloat16)], axis=0
        )
        value = jnp.zeros((1, LANES), jnp.float32)
        for c in range(POINTS):
            main = rows[pl.ds(c * 2 * LANES, LANES, stride=2), :].astype(jnp.bfloat16)
            rest = rows[pl.ds(c * 2 * LANES + 1, LANES, stride=2), :].astype(jnp.bfloat16)
            products = jnp.dot(
                jnp.concatenate([main, rest], axis=1), profile, preferred_element_type=jnp.float32
            )
            fetch(next_j, next_rows, c, 0, LANES // 2)
            diagonal = jnp.sum(jnp.where(eye, products, 0.0), axis=0, keepdims=True)
            value = value + diagonal * weight[c : c + 1, pl.ds(col, LANES)]
            fetch(next_j, next_rows, c, LANES // 2, LANES // 2)
        value = innovation[pl.ds(j, 1), :] * value
        value = jnp.where(lane + j * LANES < valid[0], value, 0.0)
        impact[pl.ds(j, 1), :] = value
        same = lax.broadcasted_iota(jnp.int32, (NI, LANES), 0) == inst[pl.ds(j, 1), :]
        part[...] += jnp.where(same, value, 0.0)

    for c in range(POINTS):
        fetch(0, oa, c, 0, LANES)

    @pl.loop(0, chunks // 2)
    def _(t):
        j = t * 2
        work(j, oa, j + 1, ob)
        work(j + 1, ob, jnp.minimum(j + 2, chunks - 1), oa)

    pltpu.make_async_remote_copy(
        src_ref=outgoing.at[pl.ds(0, ranks - 1)],
        dst_ref=received.at[pl.ds(0, ranks - 1)],
        send_sem=send_sem,
        recv_sem=recv_sem.at[0],
        device_id=peer(1),
        device_id_type=MESH,
    ).wait_send()

    rows = lax.dot_general(
        jnp.ones((8, LANES), jnp.float32),
        part[...],
        (((1,), (1,)), ((), ())),
        precision=lax.Precision.HIGHEST,
        preferred_element_type=jnp.float32,
    )
    own_rows = jnp.concatenate([rows, jnp.zeros((8, LANES - NI), jnp.float32)], axis=1)

    def share(value, slots_at, size, mine, device, base):
        slots_at[mine] = value
        shared = [
            pltpu.make_async_remote_copy(
                src_ref=slots_at.at[mine],
                dst_ref=slots_at.at[mine],
                send_sem=share_send.at[base + k],
                recv_sem=share_recv.at[base + k],
                device_id=device(lax.rem(mine + k, size)),
                device_id_type=MESH,
            )
            for k in range(1, size)
        ]
        for copy in shared:
            copy.start()
        for copy in shared:
            copy.wait()
        return jnp.sum(slots_at[...], axis=0)

    store_field.wait()
    near = share(own_rows, near_shares, ny, gy, lambda i: (gx, i), 0)
    total[...] = share(near, far_shares, nx, gx, lambda i: (i, gy), ny)[0:1, :NI]


def run(columns, valid, gradient, coupling, transport, jac, slots, weight, innovation, inst, nx, ny):
    ranks = nx * ny
    levels, rows_x, lanes = gradient.shape
    count = innovation.shape[0]
    chunks = count // LANES
    flat = gradient.reshape(levels * rows_x, lanes)
    padded = -(-levels // TAIL) * TAIL
    slots = slots.reshape(POINTS, chunks, LANES).transpose(1, 0, 2).reshape(chunks * POINTS * LANES)
    f32, bf16 = jnp.float32, jnp.bfloat16
    row_edges = pltpu.VMEM((STEPS, 2, padded, LANES), f32)
    col_edges = pltpu.VMEM((STEPS, 2, 2, rows_x, LANES), f32)
    block = pltpu.VMEM((ranks, BLOCK, LANES), bf16)
    field, impact, total = pl.pallas_call(
        whole_kernel,
        out_shape=(
            jax.ShapeDtypeStruct(flat.shape, f32),
            jax.ShapeDtypeStruct((chunks, LANES), f32),
            jax.ShapeDtypeStruct((1, NI), f32),
        ),
        in_specs=[HBM, SMEM] + [HBM] * 8,
        out_specs=(HBM, VMEM, VMEM),
        scratch_shapes=[
            pltpu.VMEM(flat.shape, f32),
            pltpu.SMEM(columns.shape, jnp.int32),
            pltpu.VMEM(flat.shape, f32),
            pltpu.VMEM(coupling.shape, f32),
            pltpu.VMEM(transport.shape, bf16),
            pltpu.VMEM(jac.shape, bf16),
            pltpu.VMEM(weight.shape, f32),
            pltpu.VMEM((chunks, LANES), f32),
            pltpu.VMEM((chunks, LANES), jnp.int32),
            pltpu.VMEM(slots.shape, jnp.int32),
            pltpu.SMEM(slots.shape, jnp.int32),
            pltpu.VMEM((2 * MAIN, 2 * MAIN), f32),
            pltpu.VMEM((2, padded, padded), bf16),
            pltpu.VMEM(flat.shape, f32),
            row_edges,
            col_edges,
            row_edges,
            col_edges,
            pltpu.VMEM((2, 2, rows_x, LANES), f32),
            pltpu.VMEM((2, 2, rows_x, LANES), f32),
            pltpu.VMEM((FRONT + rows_x * lanes * 2, LANES), f32),
            pltpu.VMEM((2 * LANES, LANES), f32),
            pltpu.VMEM((2 * LANES, LANES), f32),
            block,
            block,
            pltpu.VMEM((ranks * 2 * LANES, LANES), f32),
            pltpu.VMEM((POINTS * 2 * LANES, LANES), f32),
            pltpu.VMEM((POINTS * 2 * LANES, LANES), f32),
            pltpu.VMEM((NI, LANES), f32),
            pltpu.VMEM((ny, 8, LANES), f32),
            pltpu.VMEM((nx, 8, LANES), f32),
            pltpu.SemaphoreType.DMA((STEPS, 4)),
            pltpu.SemaphoreType.DMA((STEPS, 4)),
            pltpu.SemaphoreType.DMA,
            pltpu.SemaphoreType.DMA((ranks,)),
            pltpu.SemaphoreType.DMA((nx + ny,)),
            pltpu.SemaphoreType.DMA((nx + ny,)),
            pltpu.SemaphoreType.DMA((13,)),
        ],
        compiler_params=pltpu.CompilerParams(collective_id=1, has_side_effects=True, vmem_limit_bytes=VLIM * MIB),
        name="whole",
    )(
        columns,
        valid,
        flat,
        coupling,
        transport,
        jac,
        slots,
        weight,
        innovation.reshape(chunks, LANES),
        inst.reshape(chunks, LANES),
    )
    field, impact, total = finish(field, impact, total)
    return field.reshape(gradient.shape), impact.reshape(count), total.reshape(NI)


def finish_kernel(field, impact, total, field_out, impact_out, total_out, held, in_sem, out_sem):
    size = field.shape[0] // PIECES
    cuts = [pl.ds(i * size, size) for i in range(PIECES)]
    ins = [pltpu.make_async_copy(field.at[cut], held.at[cut], in_sem.at[i]) for i, cut in enumerate(cuts)]
    outs = [pltpu.make_async_copy(held.at[cut], field_out.at[cut], out_sem.at[i]) for i, cut in enumerate(cuts)]
    for copy in ins:
        copy.start()
    impact_out[...] = impact[...]
    total_out[...] = total[...]
    for come, go in zip(ins, outs):
        come.wait()
        go.start()
    for copy in outs:
        copy.wait()


def finish(field, impact, total):
    return pl.pallas_call(
        finish_kernel,
        out_shape=tuple(jax.ShapeDtypeStruct(a.shape, a.dtype) for a in (field, impact, total)),
        in_specs=[HBM, VMEM, VMEM],
        out_specs=(HBM, VMEM, VMEM),
        scratch_shapes=[
            pltpu.VMEM(field.shape, field.dtype),
            pltpu.SemaphoreType.DMA((PIECES,)),
            pltpu.SemaphoreType.DMA((PIECES,)),
        ],
        compiler_params=pltpu.CompilerParams(vmem_limit_bytes=VLIM * MIB),
        name="finish",
    )(field, impact, total)


def body(
    gradient,
    coupling,
    transport,
    obs_jacobian,
    send_cols,
    obs_slots,
    obs_weight,
    obs_inst,
    innovation,
    valid_count,
):
    return run(
        send_cols[0],
        valid_count,
        gradient,
        coupling,
        transport,
        obs_jacobian,
        obs_slots,
        obs_weight,
        innovation,
        obs_inst,
        lax.axis_size("gx"),
        lax.axis_size("gy"),
    )


def solution(mesh):
    placed = (
        P(None, "gx", "gy"),
        P(),
        P(None, None, "gx", "gy"),
        P(None, ("gx", "gy")),
        P(("gx", "gy"), None),
        P(None, ("gx", "gy")),
        P(None, ("gx", "gy")),
        P(("gx", "gy")),
        P(("gx", "gy")),
        P(("gx", "gy")),
    )
    return jax.shard_map(
        body,
        mesh=mesh,
        in_specs=placed,
        out_specs=(P(None, "gx", "gy"), P(("gx", "gy")), P()),
        check_vma=False,
    )
```
